32 devices in a mesh: leaf: 8 (over z, x), grid: 4 (over y, core).
Axes of the slice: x: 2, y: 2, z: 4, core: 2. Of those that a mesh axis runs over, the one named last changes fastest.
Arguments:
- rhs_rows: float32 [16384, 256], P(('leaf', 'grid')), may hold values from -6 to 6
- order: int32 [16384], P(('leaf', 'grid')), may hold values from 0 to 511, as said below
- leaf_inverse: float32 [16384, 2048], P('leaf', 'grid'), as said below
- leaf_panels: float32 [8, 4, 1024, 2048], P('leaf', None, None, 'grid'), may hold values from -0.046875 to 0.046875
- panel_mask: int32 [8, 4, 16], P('leaf', None, 'grid'), may hold values 0 or 1
- sep_rhs: float32 [8, 1024, 256], P('leaf', None, 'grid'), may hold values from -6 to 6
- sep_inverse: float32 [8, 1024, 1024], P('leaf'), as said below
- sep_panels: float32 [8, 3, 1024, 1024], P('leaf'), may hold values from -0.0625 to 0.0625
Outputs:
- leaf_solution: float32 [16384, 256], P(('leaf', 'grid'))
- sep_solution: float32 [8, 1024, 256], P('leaf', None, 'grid')
- widths: float32 [256], P('grid')
The draws below stay inside these ranges and needn't reach their ends.
Inputs may be any that keep to these rules, and one draw needn't show every extreme that they name: Each row block of 512 entries of order is a permutation of 0 .. 511. Each leaf's block of leaf_inverse is lower triangular. Each separator's block of sep_inverse is lower triangular.
All inputs are finite; a program needn't handle non-finite values. No bound on the sum of `panel_mask` on one device may be relied on, other than what follows from the above.
Results may differ from the reference program's by a relative error of at most 0.0001.
Values sent between devices are 32-bit elements; how exact they have to be, the bound alone decides.
No kernel may reach another device: no remote copies, remote signals or barrier semaphores. Data moves between devices by JAX's collectives and lax.ppermute only.
A program may use at most 192 MiB of HBM per device.

```python
import jax
import jax.numpy as jnp
import numpy as np
from jax import lax

COLUMNS = 256
LEAF_ROWS = 2048
SEP_ROWS = 1024
LEVELS = 3
TIERS = 4
BLOCKS = 32
BLOCK_ROWS = 512
SLOTS = 16
ALL_LEAF_ROWS = 16384
MASK_BLOCKS = 16
N_LEAF = 8


def lower_block(noise, diagonal, rows_total, order_size):
    local = jax.lax.broadcasted_iota(jnp.int32, (rows_total, order_size), 0) % order_size
    column = jax.lax.broadcasted_iota(jnp.int32, (rows_total, order_size), 1)
    return jnp.where(column < local, noise, jnp.where(column == local, diagonal, 0.0))


def draw_order(key, part):
    key = jax.random.fold_in(key, 3)
    keys = jax.random.split(key, BLOCKS)
    shuffled = jax.vmap(lambda single: jax.random.permutation(single, BLOCK_ROWS))(keys)
    return shuffled.reshape(-1).astype(jnp.int32)


def draw_leaf_inverse(key, part):
    key = jax.random.fold_in(key, 5)
    first, second = jax.random.split(key)
    shape = (ALL_LEAF_ROWS, LEAF_ROWS)
    noise = jax.random.normal(first, shape, jnp.float32) * (0.8 / LEAF_ROWS ** 0.5)
    diagonal = jax.random.uniform(second, shape, jnp.float32, 0.6, 1.4)
    return lower_block(noise, diagonal, ALL_LEAF_ROWS, LEAF_ROWS)


def draw_sep_inverse(key, part):
    key = jax.random.fold_in(key, 7)
    first, second = jax.random.split(key)
    shape = (N_LEAF * SEP_ROWS, SEP_ROWS)
    noise = jax.random.normal(first, shape, jnp.float32) * (0.8 / SEP_ROWS ** 0.5)
    diagonal = jax.random.uniform(second, shape, jnp.float32, 0.6, 1.4)
    return lower_block(noise, diagonal, N_LEAF * SEP_ROWS, SEP_ROWS).reshape(N_LEAF, SEP_ROWS, SEP_ROWS)


def set_ends(entries, own_key, smallest, top_value):
    index_at = [jax.random.randint(jax.random.fold_in(own_key, axis), (), 0, length) for axis, length in enumerate(entries.shape)]
    widest = entries.shape.index(max(entries.shape))
    beside = index_at[:widest] + [(index_at[widest] + 1) % entries.shape[widest]] + index_at[widest + 1:]
    return entries.at[tuple(index_at)].set(smallest).at[tuple(beside)].set(top_value)


def level_of(rng, dims, cuts, smallest, largest):
    level, own = 1.0, jax.random.fold_in(rng, 6)
    for axis_at, shards_of in cuts:
        heights = jnp.exp(jax.random.uniform(jax.random.fold_in(own, axis_at), (shards_of,), jnp.float32, smallest / len(cuts), largest / len(cuts)))
        level = level * jnp.repeat(heights, dims[axis_at] // shards_of).reshape([-1 if axis == axis_at else 1 for axis in range(len(dims))])
    return level


def gaussian(rng, dims, scale, reach, cuts=(), held_as=jnp.bfloat16):
    values = scale * jax.random.normal(rng, dims, jnp.float32)
    if cuts:
        values = values * level_of(rng, dims, cuts, -0.22, 0.18)
    return jnp.clip(values, -reach, reach).astype(held_as)


def setup_inputs(seed: int = 0) -> dict:
    seeds = jax.random.split(jax.random.key(seed), 9)
    rhs_rows = gaussian(seeds[0], (ALL_LEAF_ROWS, COLUMNS), 1.0, 6.0, ((0, 32),), jnp.float32)
    order = draw_order(jax.random.fold_in(seeds[8], 71), 0)
    leaf_inverse = draw_leaf_inverse(jax.random.fold_in(seeds[8], 71), 0)
    leaf_panels = gaussian(seeds[3], (N_LEAF, TIERS, SEP_ROWS, LEAF_ROWS), (LEAF_ROWS * N_LEAF) ** -0.5, 0.046875, ((0, 8), (3, 4)), jnp.float32)
    panel_mask = set_ends((jax.random.randint(seeds[4], (N_LEAF, TIERS, MASK_BLOCKS), 0, 4) < 3).astype(jnp.int32), jax.random.fold_in(seeds[4], 1), 0, 1)
    sep_rhs = gaussian(seeds[5], (N_LEAF, SEP_ROWS, COLUMNS), 1.0, 6.0, ((0, 8), (2, 4)), jnp.float32)
    sep_inverse = draw_sep_inverse(jax.random.fold_in(seeds[8], 71), 0)
    sep_panels = gaussian(seeds[7], (N_LEAF, LEVELS, SEP_ROWS, SEP_ROWS), (SEP_ROWS * N_LEAF) ** -0.5, 0.0625, ((0, 8),), jnp.float32)
    return {"rhs_rows": rhs_rows, "order": order, "leaf_inverse": leaf_inverse, "leaf_panels": leaf_panels, "panel_mask": panel_mask, "sep_rhs": sep_rhs, "sep_inverse": sep_inverse, "sep_panels": sep_panels}


def host_of(index, tier):
    return index // 2 ** tier * 2 ** tier + 2 ** (tier - 1) - 1

def reference(rhs_rows, order, leaf_inverse, leaf_panels, panel_mask, sep_rhs, sep_inverse, sep_panels):
    highest = lax.Precision.HIGHEST
    source = jnp.arange(BLOCKS, dtype=jnp.int32)[:, None] * BLOCK_ROWS + order.reshape(BLOCKS, BLOCK_ROWS).astype(jnp.int32)
    source = source.reshape(BLOCKS, BLOCKS, SLOTS).transpose(1, 0, 2).reshape(-1)
    permuted = rhs_rows[source]
    blocks = permuted.reshape(N_LEAF, LEAF_ROWS, COLUMNS)
    inverse = leaf_inverse.reshape(N_LEAF, LEAF_ROWS, LEAF_ROWS)
    leaf_y = jnp.einsum('nij,njk->nik', inverse, blocks, precision=highest)
    column_mask = jnp.repeat(panel_mask.astype(jnp.float32), 128, axis=2)
    leaves = np.arange(N_LEAF)
    update = jnp.zeros((N_LEAF, SEP_ROWS, COLUMNS), jnp.float32)
    for tier in range(1, TIERS + 1):
        masked = leaf_panels[:, tier - 1] * column_mask[:, tier - 1, None, :]
        contrib = jnp.einsum('nsj,njk->nsk', masked, leaf_y, precision=highest)
        update = update.at[host_of(leaves, tier)].add(contrib)
    level = np.ones(N_LEAF, dtype=np.int64)
    for bit in range(1, TIERS):
        level = level + ((leaves + 1) % 2 ** bit == 0)
    sep_y = jnp.zeros((N_LEAF, SEP_ROWS, COLUMNS), jnp.float32)
    for tier in range(1, TIERS + 1):
        hosts = leaves[level == tier]
        rhs = sep_rhs[hosts] - update[hosts]
        solved = jnp.einsum('hij,hjk->hik', sep_inverse[hosts], rhs, precision=highest)
        sep_y = sep_y.at[hosts].set(solved)
        for step in range(TIERS - tier):
            target = host_of(hosts, tier + 1 + step)
            term = jnp.einsum('hij,hjk->hik', sep_panels[hosts, step], solved, precision=highest)
            update = update.at[target].add(term)
    total = lax.optimization_barrier(jnp.sum(leaf_y * leaf_y, axis=(0, 1))) + lax.optimization_barrier(jnp.sum(sep_y * sep_y, axis=(0, 1)))
    widths = jnp.sqrt(total / (N_LEAF * (LEAF_ROWS + SEP_ROWS)) + 1e-06)
    return (leaf_y.reshape(ALL_LEAF_ROWS, COLUMNS), sep_y, widths)
```

```python
import functools

import jax
import jax.numpy as jnp
from jax import lax
from jax.experimental import pallas as pl
from jax.experimental.pallas import tpu as pltpu
from jax.sharding import PartitionSpec as P

HIGH = lax.Precision.HIGH
SMEM = pl.BlockSpec(memory_space=pltpu.SMEM)
VMEM = pl.BlockSpec(memory_space=pltpu.VMEM)
HBM = pl.BlockSpec(memory_space=pl.ANY)
PIECE = 128
MIB = 2**20


def shaped(*shape, dtype=jnp.float32):
    return jax.ShapeDtypeStruct(shape, dtype)


def cost(products):
    return pl.CostEstimate(flops=24 * products, bytes_accessed=4 * 2**20, transcendentals=0)


def limit(mebibytes):
    return pltpu.CompilerParams(vmem_limit_bytes=mebibytes * MIB)


def split(value):
    high = value.astype(jnp.bfloat16)
    return high, (value - high.astype(jnp.float32)).astype(jnp.bfloat16)


def split_wide(value):
    high = value.astype(jnp.bfloat16)
    return high, value - high.astype(jnp.float32)


def in_hbm(value):
    return pltpu.with_memory_space_constraint(value, pltpu.HBM)


def in_vmem(value):
    return pltpu.with_memory_space_constraint(value, pltpu.VMEM)


def pieces(source, held, arrived):
    copies = []
    for step in range(held.shape[0] // PIECE):
        at = pl.ds(step * PIECE, PIECE)
        copies.append(pltpu.make_async_copy(source.at[at], held.at[at], arrived.at[step]))
        copies[step].start()
    return copies


def wait(copies, rows):
    for copy in copies[rows.start // PIECE : rows.stop // PIECE]:
        copy.wait()


def whole(*shape):
    return pl.BlockSpec(shape, lambda *step: (0,) * len(shape))


def pick_kernel(order, rows, out):
    size = rows.shape[0]
    place = lax.broadcasted_iota(jnp.int32, (size, size), 0)
    chosen = jnp.where(place == order[...], 1.0, 0.0).T.astype(jnp.bfloat16)
    high, rest = split_wide(rows[...])
    middle, low = split(rest)
    value = jnp.dot(chosen, high, preferred_element_type=jnp.float32)
    value = value + jnp.dot(chosen, middle, preferred_element_type=jnp.float32)
    out[...] = value + jnp.dot(chosen, low, preferred_element_type=jnp.float32)


def pick(rows, order):
    size, columns = rows.shape
    return pl.pallas_call(
        pick_kernel,
        out_shape=shaped(size, columns),
        grid=(1,),
        in_specs=[whole(1, size), whole(size, columns)],
        out_specs=whole(size, columns),
        cost_estimate=cost(size * size * columns),
        compiler_params=limit(12),
    )(in_hbm(order.reshape(1, size)), in_hbm(rows))


def product_kernel(last_two, place, matrix, rows, *outs):
    size = rows.shape[0]
    for step in range(2):
        block = 2 + ((place[0] & 1) ^ (1 - step)) if last_two else 1 - step
        at = pl.ds(pl.multiple_of(block * size, size), size)
        value = jnp.dot(
            matrix[at], rows[...], precision=HIGH, preferred_element_type=jnp.float32
        )
        if last_two:
            outs[step][...] = value
        elif step == 0:
            outs[0][...] = value[: size // 2]
            outs[1][...] = value[size // 2 :]
        else:
            outs[2][...] = value


def two_products(place, matrix, rows, last_two):
    size, columns = rows.shape
    shapes = [size, size] if last_two else [size // 2, size // 2, size]
    return pl.pallas_call(
        functools.partial(product_kernel, last_two),
        out_shape=[shaped(count, columns) for count in shapes],
        in_specs=[SMEM, VMEM, VMEM],
        out_specs=[VMEM] * len(shapes),
        cost_estimate=cost(2 * size * size * columns),
        compiler_params=limit(8),
    )(place, in_vmem(matrix), rows)


def update_of(turned, scale, panel):
    return lax.dot_general(
        turned * scale,
        panel,
        (((1,), (1,)), ((), ())),
        precision=HIGH,
        preferred_element_type=jnp.float32,
    )


def hand_out(value, core, rows, lanes, width, given, kept):
    for mine in range(2):

        @pl.when(core == mine)
        def _(mine=mine):
            for half in range(2):
                at = (2 * half + mine) * width
                other = (2 * half + 1 - mine) * width
                kept[half, rows, lanes] = value[at : at + width]
                given[half, rows, lanes] = value[other : other + width]


def first_update_kernel(
    width, where, kept_in, in_chip, between, lowest, top, bottom, pair_top, pair_bottom, scale, panels,
    leaf_y, turned, squares, given, kept
):
    place = where[0]

    @pl.when(place == 0)
    def _():
        leaf_y[...] = lowest[...]

    @pl.when(place == 1)
    def _():
        middle = leaf_y.shape[0] // 2
        leaf_y[:middle] = top[...] + pair_top[...]
        leaf_y[middle:] = bottom[...] + pair_bottom[...]

    @pl.when(place == 2)
    def _():
        leaf_y[...] = kept_in[...] + between[...]

    @pl.when(place == 3)
    def _():
        leaf_y[...] = (kept_in[...] + in_chip[...]) + between[...]

    turned[...] = leaf_y[...].T
    value = update_of(turned[...], scale[0:1], panels[0])
    hand_out(value, place & 1, slice(None), slice(None), width, given, kept)
    own = jnp.sum(leaf_y[...] * leaf_y[...], axis=0, keepdims=True)
    squares[...] = jnp.broadcast_to(own, squares.shape)


def first_update(where, parts, scale, panels):
    size, columns = parts[0].shape
    rows = panels.shape[1]
    width = columns // 4
    halves = shaped(2, width, rows)
    return pl.pallas_call(
        functools.partial(first_update_kernel, width),
        out_shape=(
            shaped(size, columns), shaped(columns, size), shaped(8, columns), halves, halves
        ),
        in_specs=[SMEM] + [VMEM] * (len(parts) + 2),
        out_specs=(VMEM,) * 5,
        cost_estimate=cost(size * rows * columns),
        compiler_params=limit(12),
    )(where, *parts, scale, in_vmem(panels))


def second_update_kernel(width, where, turned, scale, panels, given, kept):
    every = slice(None)
    value = update_of(turned[...], scale[1:2], panels[1])
    hand_out(value, where[0] & 1, every, every, width, given, kept)


def second_update(where, turned, scale, panels):
    columns, size = turned.shape
    rows = panels.shape[1]
    width = columns // 4
    halves = shaped(2, width, rows)
    return pl.pallas_call(
        functools.partial(second_update_kernel, width),
        out_shape=(halves, halves),
        in_specs=[SMEM] + [VMEM] * 3,
        out_specs=(VMEM, VMEM),
        cost_estimate=cost(size * rows * columns),
        compiler_params=limit(8),
    )(where, turned, scale, in_vmem(panels))


def later_update_kernel(width, where, squares, turned, scale, panels, given, kept):
    core = where[0] & 1
    tiers = panels.shape[0]
    for tier in range(2, tiers):
        value = update_of(turned[...], scale[tier : tier + 1], panels[tier])
        rows = slice((tier - 2) * width, (tier - 1) * width)
        hand_out(value, core, rows, slice(None), width, given, kept)
    at = (tiers - 2) * width
    for refs, of in ((given, 1 - core), (kept, core)):
        refs[:, at:, :] = jnp.zeros((2, 8, refs.shape[2]), jnp.float32)
        for half in range(2):
            pair = squares[:, 2 * width * half : 2 * width * (half + 1)]
            pair = jnp.where(of == 0, pair, pltpu.roll(pair, width, 1))
            refs[half, at:, 0 : 2 * width] = pair


def later_updates(where, squares, turned, scale, panels):
    columns, size = turned.shape
    tiers, rows = panels.shape[:2]
    width = columns // 4
    halves = shaped(2, (tiers - 2) * width + 8, rows)
    return pl.pallas_call(
        functools.partial(later_update_kernel, width),
        out_shape=(halves, halves),
        in_specs=[SMEM] + [VMEM] * 4,
        out_specs=(VMEM, VMEM),
        cost_estimate=cost(1),
        compiler_params=limit(12),
    )(where, squares, turned, scale, in_vmem(panels))


def chip_sum_kernel(where, kept, got, own, away):
    half = where[0] >> 1
    own[...] = kept[half] + got[half]
    away[...] = kept[1 - half] + got[1 - half]


def chip_sum(where, kept, got):
    shape = shaped(*kept.shape[1:])
    return pl.pallas_call(
        chip_sum_kernel,
        out_shape=(shape, shape),
        in_specs=[SMEM, VMEM, VMEM],
        out_specs=(VMEM, VMEM),
        cost_estimate=cost(1),
        compiler_params=limit(6),
    )(where, kept, got)


def prepare_kernel(
    inverse, panels, out, wide, direct_high, direct_low, high, low, inverse_arrived, panel_arrived, gone
):
    rows = high.shape[0]
    block = rows // 4
    copies = pieces(inverse.at[0], wide.at[0], inverse_arrived)
    pieces(panels.at[0, 0], wide.at[1], panel_arrived)
    for at in range(0, rows, block):
        part = slice(at, at + block)
        wait(copies, part)
        high[part], low[part] = split(wide[0, part])
    sent = [
        pltpu.make_async_copy(source, out.at[2 + step], gone.at[step])
        for step, source in enumerate((high, low))
    ]
    for copy in sent:
        copy.start()

    def part_sent(step):
        part = pl.ds(pl.multiple_of(step * block, block), block)
        return [
            pltpu.make_async_copy(source.at[part], out.at[which, part], gone.at[2 + which])
            for which, source in enumerate((direct_high, direct_low))
        ]

    @pl.loop(0, 4)
    def _(step):
        part = pl.ds(pl.multiple_of(step * block, block), block)
        for piece in range(block // PIECE):
            at = pl.ds(pl.multiple_of(step * block + piece * PIECE, PIECE), PIECE)
            pltpu.make_async_copy(
                panels.at[0, 0, at], wide.at[1, at], panel_arrived.at[step * (block // PIECE) + piece]
            ).wait()
        panel_high, panel_low = split(wide[1, part])
        for at in range(0, rows, block):
            lanes = slice(at, at + block)
            both = high[at:, lanes]
            value = jnp.dot(panel_high[:, at:], both, preferred_element_type=jnp.float32)
            value = value + jnp.dot(panel_low[:, at:], both, preferred_element_type=jnp.float32)
            value = value + jnp.dot(
                panel_high[:, at:], low[at:, lanes], preferred_element_type=jnp.float32
            )
            direct_high[part, lanes], direct_low[part, lanes] = split(value)

        @pl.when(step > 0)
        def _():
            for copy in part_sent(step - 1):
                copy.wait()

        for copy in part_sent(step):
            copy.start()

    for copy in sent + part_sent(3):
        copy.wait()


def prepared(sep_inverse, sep_panels):
    rows = sep_inverse.shape[1]
    return pl.pallas_call(
        prepare_kernel,
        out_shape=pltpu.HBM((4, rows, rows), jnp.bfloat16),
        in_specs=[HBM] * 2,
        out_specs=HBM,
        scratch_shapes=[pltpu.VMEM((2, rows, rows), jnp.float32)]
        + [pltpu.VMEM((rows, rows), jnp.bfloat16)] * 4
        + [
            pltpu.SemaphoreType.DMA((rows // PIECE,)),
            pltpu.SemaphoreType.DMA((rows // PIECE,)),
            pltpu.SemaphoreType.DMA((4,)),
        ],
        cost_estimate=cost(rows**3),
        compiler_params=limit(24),
    )(in_hbm(sep_inverse), in_hbm(sep_panels))


def load_kernel(halves, panels, halves_out, panels_out, arrived):
    copies = [(panels.at[0, step], panels_out.at[step]) for step in range(panels_out.shape[0])]
    copies += [(halves.at[step], halves_out.at[step]) for step in range(4)]
    copies = [
        pltpu.make_async_copy(source, target, arrived.at[step])
        for step, (source, target) in enumerate(copies)
    ]
    for copy in copies:
        copy.start()
    for copy in copies:
        copy.wait()


def loaded(halves, leaf_panels):
    return pl.pallas_call(
        load_kernel,
        out_shape=(
            pltpu.VMEM(halves.shape, jnp.bfloat16),
            pltpu.VMEM(leaf_panels.shape[1:], jnp.float32),
        ),
        in_specs=[HBM] * 2,
        out_specs=(VMEM,) * 2,
        scratch_shapes=[pltpu.SemaphoreType.DMA((4 + leaf_panels.shape[1],))],
        cost_estimate=cost(1),
        compiler_params=limit(4),
    )(in_hbm(halves), in_hbm(leaf_panels))


def load_panel_kernel(panels, out, arrived):
    copies = pieces(panels.at[0, 1], out, arrived)
    wait(copies, slice(0, out.shape[0]))


def loaded_panel(panels):
    rows = panels.shape[2]
    return pl.pallas_call(
        load_panel_kernel,
        out_shape=pltpu.VMEM(panels.shape[2:], jnp.float32),
        in_specs=[HBM],
        out_specs=VMEM,
        scratch_shapes=[pltpu.SemaphoreType.DMA((rows // PIECE,))],
        cost_estimate=cost(1),
        compiler_params=limit(4),
    )(in_hbm(panels))


def operands(value):
    width = value.shape[1] // 2
    lane = lax.broadcasted_iota(jnp.int32, value.shape, 1)
    high = value.astype(jnp.bfloat16)
    as_wide = high.astype(jnp.float32)
    return jnp.where(lane < width, as_wide, value - as_wide).astype(jnp.bfloat16), high


def applied(matrix_high, matrix_low, both, high):
    first = jnp.dot(matrix_high, both, preferred_element_type=jnp.float32)
    second = jnp.dot(matrix_low, high, preferred_element_type=jnp.float32)
    return (first + pltpu.roll(first, first.shape[1] // 2, 1)) + second


def doubled(value):
    return jnp.concatenate([value, value], axis=0).T


def left_of(own_rhs, parts):
    whole_parts = [part[...] for part in parts if part.shape == own_rhs.shape]
    halves = [part[...] for part in parts if part.shape != own_rhs.shape]
    total = whole_parts[0]
    for part in whole_parts[1:]:
        total = total + part
    if halves:
        total = total + jnp.concatenate(halves, axis=0)
    return own_rhs[...] - total


def direct_kernel(count, own_rhs, halves, *refs):
    parts, (left, term) = refs[:count], refs[count:]
    left[...] = left_of(own_rhs, parts)
    value = applied(halves[0], halves[1], *operands(doubled(left[...])))
    term[...] = value.T[: term.shape[0]]


def direct(own_rhs, halves, parts):
    width, rows = own_rhs.shape
    return pl.pallas_call(
        functools.partial(direct_kernel, len(parts)),
        out_shape=(shaped(width, rows), shaped(width, rows)),
        in_specs=[VMEM] * (2 + len(parts)),
        out_specs=(VMEM, VMEM),
        cost_estimate=cost(rows**2 * 4096),
        compiler_params=limit(8),
    )(own_rhs, in_vmem(halves), *parts)


def tail_of(copies, held, both, high, width, out):
    rows = held.shape[0]
    block = rows // 4
    for at in range(0, rows, block):
        part = slice(at, at + block)
        if copies:
            wait(copies, part)
        out[:width, part] = applied(*split(held[part]), both, high).T[:width]


def with_squares(out, width, squares):
    out[width:, :] = jnp.zeros((8, out.shape[1]), jnp.float32)
    out[width:, : squares.shape[1]] = squares[...]


def solve_kernel(tier, last, with_tail, where, left, halves, solved, *refs):
    panel, refs = refs[0] if with_tail else None, refs[with_tail:]
    out, squares, kept, *sent = refs
    width = left.shape[0]
    value = applied(halves[2], halves[3], *operands(doubled(left[...])))
    mine = value.T[:width]
    kept[...] = value

    @pl.when(where[2] == tier)
    def _():
        out[...] = mine

    @pl.when(where[2] != tier)
    def _():
        out[...] = solved[...]

    own = jnp.sum(value * value, axis=0, keepdims=True)
    squares[...] = jnp.broadcast_to(own, squares.shape)
    if sent:
        tail_of(None, panel, *operands(value), width, sent[0])
        if last:
            with_squares(sent[0], width, squares)


def solve(where, tier, left, halves, solved, panel=None, last=False):
    width, rows = left.shape
    with_tail = panel is not None
    return pl.pallas_call(
        functools.partial(solve_kernel, tier, last, with_tail),
        out_shape=[shaped(width, rows), shaped(8, 2 * width), shaped(rows, 2 * width)]
        + [shaped(width + 8 * last, rows)] * with_tail,
        in_specs=[SMEM] + [VMEM] * (3 + with_tail),
        out_specs=[VMEM] * (3 + with_tail),
        cost_estimate=cost(1),
        compiler_params=limit(8),
    )(where, left, in_vmem(halves), solved, *([in_vmem(panel)] if with_tail else []))


def tails_kernel(value, squares, panels, *refs):
    sent, (held, arrived) = refs[:-2], refs[-2:]
    width = squares.shape[1] // 2
    copies = [
        pieces(panels.at[0, 2 + step], held.at[step], arrived.at[step])
        for step in range(held.shape[0])
    ]
    both, high = operands(value[...])
    for step, out in enumerate(sent):
        tail_of(copies[step], held.at[step], both, high, width, out)
    with_squares(sent[-1], width, squares)


def more_tails(value, squares, panels, count):
    rows = value.shape[0]
    width = squares.shape[1] // 2
    shapes = [(width + 8 * (step == count - 1), rows) for step in range(count)]
    return pl.pallas_call(
        tails_kernel,
        out_shape=[shaped(*shape) for shape in shapes],
        in_specs=[VMEM, VMEM, HBM],
        out_specs=[VMEM] * count,
        scratch_shapes=[
            pltpu.VMEM((count, rows, rows), jnp.float32),
            pltpu.SemaphoreType.DMA((count, rows // PIECE)),
        ],
        cost_estimate=cost(1),
        compiler_params=limit(8 + 4 * count),
    )(value, squares, in_hbm(panels))


def last_kernel(leaves, count, where, own_rhs, halves, squares, got, first, second, kept, widths):
    left = left_of(own_rhs, (first, second))
    value = applied(halves[2], halves[3], *operands(doubled(left)))
    kept[...] = value
    total = (squares[...] + got[...]) + jnp.sum(value * value, axis=0, keepdims=True)
    value = jnp.sqrt(total / count + 1e-06)
    widths[...] = jnp.where(where[1] == leaves - 1, value, 0.0)


def last(leaves, count, where, own_rhs, halves, squares, got, parts):
    width, rows = own_rhs.shape
    return pl.pallas_call(
        functools.partial(last_kernel, leaves, count),
        out_shape=(shaped(rows, 2 * width), shaped(*squares.shape)),
        in_specs=[SMEM] + [VMEM] * 6,
        out_specs=(VMEM, VMEM),
        cost_estimate=cost(1),
        compiler_params=limit(8),
    )(where, own_rhs, in_vmem(halves), squares, got, *parts)


def settle_kernel(tiers, where, solved, value, out):
    width = out.shape[0]

    @pl.when(where[2] == tiers)
    def _():
        out[...] = value[...].T[:width]

    @pl.when(where[2] != tiers)
    def _():
        out[...] = solved[...]


def settled(tiers, where, solved, value):
    return pl.pallas_call(
        functools.partial(settle_kernel, tiers),
        out_shape=shaped(*solved.shape),
        in_specs=[SMEM, VMEM, VMEM],
        out_specs=VMEM,
        cost_estimate=cost(1),
        compiler_params=limit(6),
    )(where, solved, value)


def local(rhs_rows, order, leaf_inverse, leaf_panels, panel_mask, sep_rhs, sep_inverse, sep_panels):
    n_leaf = lax.axis_size("leaf")
    n_grid = lax.axis_size("grid")
    tiers = leaf_panels.shape[1]
    block_rows, columns = rhs_rows.shape
    block_count = n_leaf * n_grid
    sep_rows = sep_rhs.shape[1]
    width = columns // n_grid
    leaf = lax.axis_index("leaf").astype(jnp.int32)
    grid = lax.axis_index("grid").astype(jnp.int32)
    level = jnp.ones((), jnp.int32)
    for bit in range(1, tiers):
        level = level + ((leaf + 1) & (2**bit - 1) == 0).astype(jnp.int32)
    where = jnp.stack([grid, leaf, level])
    scale = jnp.repeat(panel_mask[0].astype(jnp.float32), 128, axis=1)

    picked = pick(rhs_rows, order)
    picked, where = lax.optimization_barrier((picked, where))
    moved = lax.all_to_all(
        picked.reshape(block_count, block_rows // block_count, columns),
        ("leaf", "grid"),
        split_axis=0,
        concat_axis=0,
        tiled=True,
    )
    permuted = moved.reshape(block_rows, columns)

    _, inverse, own_panels = lax.optimization_barrier((picked, sep_inverse, sep_panels))
    halves = prepared(inverse, own_panels)
    permuted, halves = lax.optimization_barrier((permuted, halves))

    given, kept = two_products(where, leaf_inverse, permuted, True)
    in_chip = lax.ppermute(given, "grid", [(0, 1), (1, 0), (2, 3)])
    onward = kept + in_chip
    onward, permuted, halves = lax.optimization_barrier((onward, permuted, halves))
    between = lax.ppermute(onward, "grid", [(0, 2), (1, 3)])
    *low_block, lowest = two_products(where, leaf_inverse, permuted, False)
    from_pair = [lax.ppermute(part, "grid", [(0, 1)]) for part in low_block]
    halves, panels = loaded(halves, leaf_panels)

    leaf_y, turned, squares, given, kept = first_update(
        where, (kept, in_chip, between, lowest, *low_block, *from_pair), scale, panels
    )
    swap = [(0, 1), (1, 0), (2, 3), (3, 2)]
    over = [(0, 2), (1, 3), (2, 0), (3, 1)]
    got = lax.ppermute(given, "grid", swap)
    given, other = second_update(where, turned, scale, panels)
    own, away = chip_sum(where, kept, got)
    away, given, turned = lax.optimization_barrier((away, given, turned))
    got = lax.ppermute(away, "grid", over)
    second, away = chip_sum(where, other, lax.ppermute(given, "grid", swap))
    given, kept = later_updates(where, squares, turned, scale, panels)
    got, away, given = lax.optimization_barrier((got, away, given))
    mine = own + got
    following = second + lax.ppermute(away, "grid", over)
    own, away = chip_sum(where, kept, lax.ppermute(given, "grid", swap))
    pairs = [(base + 1, base) for base in range(0, n_leaf, 2)]
    own, own_panels = lax.optimization_barrier((own, sep_panels))
    next_panel = loaded_panel(own_panels)
    got, own, next_panel = lax.optimization_barrier(
        (lax.ppermute(mine, "leaf", pairs), own, next_panel)
    )
    parts = [mine, got]
    edges = [(step * width, (step + 1) * width) for step in range(tiers - 2)]
    edges[-1] = (edges[-1][0], own.shape[0])
    rest = [
        own[start:stop] + lax.ppermute(away[start:stop], "grid", over) for start, stop in edges
    ]

    own_rhs = sep_rhs[0].T
    solved = jnp.zeros_like(own_rhs)
    waiting = []
    for tier in range(1, tiers):
        size = 2**tier
        direct_left, direct_right, early, onward, aside = [], [], [], [], []
        for base in range(0, n_leaf, size):
            host, end = (base + size // 2 - 1, base + size - 1)
            parent = base // (2 * size) * 2 * size + size - 1
            onward.append((host, end))
            if end == parent:
                direct_left.append((host, parent))
            else:
                direct_right.append((host, parent))
                early.append((end, parent))
                aside.append((host, end))
        left, term = direct(own_rhs, halves, parts)
        count = len(rest)
        solved, own, *more = solve(
            where, tier, left, halves, solved, next_panel if count else None, count == 1
        )
        if waiting:
            _, following, *waiting = lax.optimization_barrier((left, following, *waiting))
            rest = [
                other + lax.ppermute(other + tail, "leaf", before)
                for other, tail in zip(rest, waiting)
            ]
        if count:
            value, tail = more
            next_early = lax.ppermute(following, "leaf", early)
            term = following + term
            from_left = lax.ppermute(term, "leaf", direct_left)
            parts = [following, next_early, from_left]
            if tier == 1:
                turn = lax.ppermute(term[width // 2 :], "leaf", aside)
                parts.append(lax.ppermute(term[: width // 2], "leaf", direct_right))
                parts.append(lax.ppermute(turn, "leaf", early))
            else:
                parts.append(lax.ppermute(term, "leaf", direct_right))
            following = rest[0] + lax.ppermute(rest[0] + tail, "leaf", onward)
            rest = rest[1:]
            waiting = []
            if count > 1:
                value, _ = lax.optimization_barrier((value, from_left))
                waiting = more_tails(value, own, sep_panels, count - 1)
                parts[1], *waiting = lax.optimization_barrier((parts[1], *waiting))
            before = onward
        else:
            squares = following[width:, : 2 * width]
            following = following[:width]
            parts = [following, lax.ppermute(following + term, "leaf", direct_left)]
            got = lax.ppermute(squares + own, "leaf", direct_left)
    value, widths = last(
        n_leaf,
        n_leaf * (block_rows * n_grid + sep_rows),
        where,
        own_rhs,
        halves,
        squares,
        got,
        parts,
    )
    solved = settled(tiers, where, solved, value)
    step = n_leaf
    while step > 1:
        half_step = step // 2
        steps = [(end, end - half_step) for end in range(step - 1, n_leaf, step)]
        widths = widths + lax.ppermute(widths, "leaf", steps)
        step = half_step
    return (leaf_y, solved.T[None], widths[0, :width])


def solution(mesh):
    placed = (
        P(("leaf", "grid"), None),
        P(("leaf", "grid")),
        P("leaf", "grid"),
        P("leaf", None, None, "grid"),
        P("leaf", None, "grid"),
        P("leaf", None, "grid"),
        P("leaf", None, None),
        P("leaf", None, None, None),
    )
    return jax.shard_map(
        local,
        mesh=mesh,
        in_specs=placed,
        out_specs=(P(("leaf", "grid"), None), P("leaf", None, "grid"), P("grid")),
        check_vma=False,
    )
```

```python
import functools

import jax
import jax.numpy as jnp
from jax import lax
from jax.experimental import pallas as pl
from jax.experimental.pallas import tpu as pltpu
from jax.sharding import PartitionSpec as P

HIGH = lax.Precision.HIGH
SMEM = pl.BlockSpec(memory_space=pltpu.SMEM)
VMEM = pl.BlockSpec(memory_space=pltpu.VMEM)
HBM = pl.BlockSpec(memory_space=pl.ANY)
PIECE = 128
MIB = 2**20


def shaped(*shape, dtype=jnp.float32):
    return jax.ShapeDtypeStruct(shape, dtype)


def cost(products):
    return pl.CostEstimate(flops=24 * products, bytes_accessed=4 * 2**20, transcendentals=0)


def limit(mebibytes):
    return pltpu.CompilerParams(vmem_limit_bytes=mebibytes * MIB)


def split(value):
    high = value.astype(jnp.bfloat16)
    return high, (value - high.astype(jnp.float32)).astype(jnp.bfloat16)


def split_wide(value):
    high = value.astype(jnp.bfloat16)
    return high, value - high.astype(jnp.float32)


def in_hbm(value):
    return pltpu.with_memory_space_constraint(value, pltpu.HBM)


def in_vmem(value):
    return pltpu.with_memory_space_constraint(value, pltpu.VMEM)


def pieces(source, held, arrived):
    copies = []
    for step in range(held.shape[0] // PIECE):
        at = pl.ds(step * PIECE, PIECE)
        copies.append(pltpu.make_async_copy(source.at[at], held.at[at], arrived.at[step]))
        copies[step].start()
    return copies


def wait(copies, rows):
    for copy in copies[rows.start // PIECE : rows.stop // PIECE]:
        copy.wait()


def whole(*shape):
    return pl.BlockSpec(shape, lambda *step: (0,) * len(shape))


def pick_kernel(order, rows, out):
    size = rows.shape[0]
    place = lax.broadcasted_iota(jnp.int32, (size, size), 0)
    chosen = jnp.where(place == order[...], 1.0, 0.0).T.astype(jnp.bfloat16)
    high, rest = split_wide(rows[...])
    middle, low = split(rest)
    value = jnp.dot(chosen, high, preferred_element_type=jnp.float32)
    value = value + jnp.dot(chosen, middle, preferred_element_type=jnp.float32)
    out[...] = value + jnp.dot(chosen, low, preferred_element_type=jnp.float32)


def pick(rows, order):
    size, columns = rows.shape
    return pl.pallas_call(
        pick_kernel,
        out_shape=shaped(size, columns),
        grid=(1,),
        in_specs=[whole(1, size), whole(size, columns)],
        out_specs=whole(size, columns),
        cost_estimate=cost(size * size * columns),
        compiler_params=limit(12),
    )(in_hbm(order.reshape(1, size)), in_hbm(rows))


def product_kernel(last_two, place, matrix, rows, *outs):
    size = rows.shape[0]
    for step in range(2):
        block = 2 + ((place[0] & 1) ^ (1 - step)) if last_two else 1 - step
        at = pl.ds(pl.multiple_of(block * size, size), size)
        value = jnp.dot(
            matrix[at], rows[...], precision=HIGH, preferred_element_type=jnp.float32
        )
        if last_two:
            outs[step][...] = value
        elif step == 0:
            outs[0][...] = value[: size // 2]
            outs[1][...] = value[size // 2 :]
        else:
            outs[2][...] = value


def two_products(place, matrix, rows, last_two):
    size, columns = rows.shape
    shapes = [size, size] if last_two else [size // 2, size // 2, size]
    return pl.pallas_call(
        functools.partial(product_kernel, last_two),
        out_shape=[shaped(count, columns) for count in shapes],
        in_specs=[SMEM, VMEM, VMEM],
        out_specs=[VMEM] * len(shapes),
        cost_estimate=cost(2 * size * size * columns),
        compiler_params=limit(8),
    )(place, in_vmem(matrix), rows)


def update_of(turned, scale, panel):
    return lax.dot_general(
        turned * scale,
        panel,
        (((1,), (1,)), ((), ())),
        precision=HIGH,
        preferred_element_type=jnp.float32,
    )


def hand_out(value, core, rows, lanes, width, given, kept):
    for mine in range(2):

        @pl.when(core == mine)
        def _(mine=mine):
            for half in range(2):
                at = (2 * half + mine) * width
                other = (2 * half + 1 - mine) * width
                kept[half, rows, lanes] = value[at : at + width]
                given[half, rows, lanes] = value[other : other + width]


def first_update_kernel(
    width, where, kept_in, in_chip, between, lowest, top, bottom, pair_top, pair_bottom, scale, panels,
    leaf_y, turned, squares, given, kept
):
    place = where[0]

    @pl.when(place == 0)
    def _():
        leaf_y[...] = lowest[...]

    @pl.when(place == 1)
    def _():
        middle = leaf_y.shape[0] // 2
        leaf_y[:middle] = top[...] + pair_top[...]
        leaf_y[middle:] = bottom[...] + pair_bottom[...]

    @pl.when(place == 2)
    def _():
        leaf_y[...] = kept_in[...] + between[...]

    @pl.when(place == 3)
    def _():
        leaf_y[...] = (kept_in[...] + in_chip[...]) + between[...]

    turned[...] = leaf_y[...].T
    value = update_of(turned[...], scale[0:1], panels[0])
    hand_out(value, place & 1, slice(None), slice(None), width, given, kept)
    own = jnp.sum(leaf_y[...] * leaf_y[...], axis=0, keepdims=True)
    squares[...] = jnp.broadcast_to(own, squares.shape)


def first_update(where, parts, scale, panels):
    size, columns = parts[0].shape
    rows = panels.shape[1]
    width = columns // 4
    halves = shaped(2, width, rows)
    return pl.pallas_call(
        functools.partial(first_update_kernel, width),
        out_shape=(
            shaped(size, columns), shaped(columns, size), shaped(8, columns), halves, halves
        ),
        in_specs=[SMEM] + [VMEM] * (len(parts) + 2),
        out_specs=(VMEM,) * 5,
        cost_estimate=cost(size * rows * columns),
        compiler_params=limit(12),
    )(where, *parts, scale, in_vmem(panels))


def second_update_kernel(width, where, turned, scale, panels, given, kept):
    every = slice(None)
    value = update_of(turned[...], scale[1:2], panels[1])
    hand_out(value, where[0] & 1, every, every, width, given, kept)


def second_update(where, turned, scale, panels):
    columns, size = turned.shape
    rows = panels.shape[1]
    width = columns // 4
    halves = shaped(2, width, rows)
    return pl.pallas_call(
        functools.partial(second_update_kernel, width),
        out_shape=(halves, halves),
        in_specs=[SMEM] + [VMEM] * 3,
        out_specs=(VMEM, VMEM),
        cost_estimate=cost(size * rows * columns),
        compiler_params=limit(8),
    )(where, turned, scale, in_vmem(panels))


def later_update_kernel(width, where, squares, turned, scale, panels, given, kept):
    core = where[0] & 1
    tiers = panels.shape[0]
    for tier in range(2, tiers):
        value = update_of(turned[...], scale[tier : tier + 1], panels[tier])
        rows = slice((tier - 2) * width, (tier - 1) * width)
        hand_out(value, core, rows, slice(None), width, given, kept)
    at = (tiers - 2) * width
    for refs, of in ((given, 1 - core), (kept, core)):
        refs[:, at:, :] = jnp.zeros((2, 8, refs.shape[2]), jnp.float32)
        for half in range(2):
            pair = squares[:, 2 * width * half : 2 * width * (half + 1)]
            pair = jnp.where(of == 0, pair, pltpu.roll(pair, width, 1))
            refs[half, at:, 0 : 2 * width] = pair


def later_updates(where, squares, turned, scale, panels):
    columns, size = turned.shape
    tiers, rows = panels.shape[:2]
    width = columns // 4
    halves = shaped(2, (tiers - 2) * width + 8, rows)
    return pl.pallas_call(
        functools.partial(later_update_kernel, width),
        out_shape=(halves, halves),
        in_specs=[SMEM] + [VMEM] * 4,
        out_specs=(VMEM, VMEM),
        cost_estimate=cost(1),
        compiler_params=limit(12),
    )(where, squares, turned, scale, in_vmem(panels))


def chip_sum_kernel(where, kept, got, own, away):
    half = where[0] >> 1
    own[...] = kept[half] + got[half]
    away[...] = kept[1 - half] + got[1 - half]


def chip_sum(where, kept, got):
    shape = shaped(*kept.shape[1:])
    return pl.pallas_call(
        chip_sum_kernel,
        out_shape=(shape, shape),
        in_specs=[SMEM, VMEM, VMEM],
        out_specs=(VMEM, VMEM),
        cost_estimate=cost(1),
        compiler_params=limit(6),
    )(where, kept, got)


def prepare_kernel(
    inverse, panels, out, wide, direct_high, direct_low, high, low, inverse_arrived, panel_arrived, gone
):
    rows = high.shape[0]
    block = rows // 4
    copies = pieces(inverse.at[0], wide.at[0], inverse_arrived)
    pieces(panels.at[0, 0], wide.at[1], panel_arrived)
    for at in range(0, rows, block):
        part = slice(at, at + block)
        wait(copies, part)
        high[part], low[part] = split(wide[0, part])
    sent = [
        pltpu.make_async_copy(source, out.at[2 + step], gone.at[step])
        for step, source in enumerate((high, low))
    ]
    for copy in sent:
        copy.start()

    def part_sent(step):
        part = pl.ds(pl.multiple_of(step * block, block), block)
        return [
            pltpu.make_async_copy(source.at[part], out.at[which, part], gone.at[2 + which])
            for which, source in enumerate((direct_high, direct_low))
        ]

    @pl.loop(0, 4)
    def _(step):
        part = pl.ds(pl.multiple_of(step * block, block), block)
        for piece in range(block // PIECE):
            at = pl.ds(pl.multiple_of(step * block + piece * PIECE, PIECE), PIECE)
            pltpu.make_async_copy(
                panels.at[0, 0, at], wide.at[1, at], panel_arrived.at[step * (block // PIECE) + piece]
            ).wait()
        panel_high, panel_low = split(wide[1, part])
        for at in range(0, rows, block):
            lanes = slice(at, at + block)
            both = high[at:, lanes]
            value = jnp.dot(panel_high[:, at:], both, preferred_element_type=jnp.float32)
            value = value + jnp.dot(panel_low[:, at:], both, preferred_element_type=jnp.float32)
            value = value + jnp.dot(
                panel_high[:, at:], low[at:, lanes], preferred_element_type=jnp.float32
            )
            direct_high[part, lanes], direct_low[part, lanes] = split(value)

        @pl.when(step > 0)
        def _():
            for copy in part_sent(step - 1):
                copy.wait()

        for copy in part_sent(step):
            copy.start()

    for copy in sent + part_sent(3):
        copy.wait()


def prepared(sep_inverse, sep_panels):
    rows = sep_inverse.shape[1]
    return pl.pallas_call(
        prepare_kernel,
        out_shape=pltpu.HBM((4, rows, rows), jnp.bfloat16),
        in_specs=[HBM] * 2,
        out_specs=HBM,
        scratch_shapes=[pltpu.VMEM((2, rows, rows), jnp.float32)]
        + [pltpu.VMEM((rows, rows), jnp.bfloat16)] * 4
        + [
            pltpu.SemaphoreType.DMA((rows // PIECE,)),
            pltpu.SemaphoreType.DMA((rows // PIECE,)),
            pltpu.SemaphoreType.DMA((4,)),
        ],
        cost_estimate=cost(rows**3),
        compiler_params=limit(24),
    )(in_hbm(sep_inverse), in_hbm(sep_panels))


def load_kernel(halves, panels, halves_out, panels_out, arrived):
    copies = [(panels.at[0, step], panels_out.at[step]) for step in range(panels_out.shape[0])]
    copies += [(halves.at[step], halves_out.at[step]) for step in range(4)]
    copies = [
        pltpu.make_async_copy(source, target, arrived.at[step])
        for step, (source, target) in enumerate(copies)
    ]
    for copy in copies:
        copy.start()
    for copy in copies:
        copy.wait()


def loaded(halves, leaf_panels):
    return pl.pallas_call(
        load_kernel,
        out_shape=(
            pltpu.VMEM(halves.shape, jnp.bfloat16),
            pltpu.VMEM(leaf_panels.shape[1:], jnp.float32),
        ),
        in_specs=[HBM] * 2,
        out_specs=(VMEM,) * 2,
        scratch_shapes=[pltpu.SemaphoreType.DMA((4 + leaf_panels.shape[1],))],
        cost_estimate=cost(1),
        compiler_params=limit(4),
    )(in_hbm(halves), in_hbm(leaf_panels))


def load_panel_kernel(panels, out, arrived):
    copies = pieces(panels.at[0, 1], out, arrived)
    wait(copies, slice(0, out.shape[0]))


def loaded_panel(panels):
    rows = panels.shape[2]
    return pl.pallas_call(
        load_panel_kernel,
        out_shape=pltpu.VMEM(panels.shape[2:], jnp.float32),
        in_specs=[HBM],
        out_specs=VMEM,
        scratch_shapes=[pltpu.SemaphoreType.DMA((rows // PIECE,))],
        cost_estimate=cost(1),
        compiler_params=limit(4),
    )(in_hbm(panels))


def operands(value):
    width = value.shape[1] // 2
    lane = lax.broadcasted_iota(jnp.int32, value.shape, 1)
    high = value.astype(jnp.bfloat16)
    as_wide = high.astype(jnp.float32)
    return jnp.where(lane < width, as_wide, value - as_wide).astype(jnp.bfloat16), high


def applied(matrix_high, matrix_low, both, high):
    first = jnp.dot(matrix_high, both, preferred_element_type=jnp.float32)
    second = jnp.dot(matrix_low, high, preferred_element_type=jnp.float32)
    return (first + pltpu.roll(first, first.shape[1] // 2, 1)) + second


def doubled(value):
    return jnp.concatenate([value, value], axis=0).T


def left_of(own_rhs, parts):
    total = parts[0][...]
    for part in parts[1:]:
        total = total + part[...]
    return own_rhs[...] - total


def direct_kernel(count, own_rhs, halves, *refs):
    parts, (left, term) = refs[:count], refs[count:]
    left[...] = left_of(own_rhs, parts)
    value = applied(halves[0], halves[1], *operands(doubled(left[...])))
    term[...] = value.T[: term.shape[0]]


def direct(own_rhs, halves, parts):
    width, rows = own_rhs.shape
    return pl.pallas_call(
        functools.partial(direct_kernel, len(parts)),
        out_shape=(shaped(width, rows), shaped(width, rows)),
        in_specs=[VMEM] * (2 + len(parts)),
        out_specs=(VMEM, VMEM),
        cost_estimate=cost(rows**2 * 4096),
        compiler_params=limit(8),
    )(own_rhs, in_vmem(halves), *parts)


def tail_of(copies, held, both, high, width, out):
    rows = held.shape[0]
    block = rows // 4
    for at in range(0, rows, block):
        part = slice(at, at + block)
        if copies:
            wait(copies, part)
        out[:width, part] = applied(*split(held[part]), both, high).T[:width]


def with_squares(out, width, squares):
    out[width:, :] = jnp.zeros((8, out.shape[1]), jnp.float32)
    out[width:, : squares.shape[1]] = squares[...]


def solve_kernel(tier, last, with_tail, where, left, halves, solved, *refs):
    panel, refs = refs[0] if with_tail else None, refs[with_tail:]
    out, squares, kept, *sent = refs
    width = left.shape[0]
    value = applied(halves[2], halves[3], *operands(doubled(left[...])))
    mine = value.T[:width]
    kept[...] = value

    @pl.when(where[2] == tier)
    def _():
        out[...] = mine

    @pl.when(where[2] != tier)
    def _():
        out[...] = solved[...]

    own = jnp.sum(value * value, axis=0, keepdims=True)
    squares[...] = jnp.broadcast_to(own, squares.shape)
    if sent:
        tail_of(None, panel, *operands(value), width, sent[0])
        if last:
            with_squares(sent[0], width, squares)


def solve(where, tier, left, halves, solved, panel=None, last=False):
    width, rows = left.shape
    with_tail = panel is not None
    return pl.pallas_call(
        functools.partial(solve_kernel, tier, last, with_tail),
        out_shape=[shaped(width, rows), shaped(8, 2 * width), shaped(rows, 2 * width)]
        + [shaped(width + 8 * last, rows)] * with_tail,
        in_specs=[SMEM] + [VMEM] * (3 + with_tail),
        out_specs=[VMEM] * (3 + with_tail),
        cost_estimate=cost(1),
        compiler_params=limit(8),
    )(where, left, in_vmem(halves), solved, *([in_vmem(panel)] if with_tail else []))


def tails_kernel(value, squares, panels, *refs):
    sent, (held, arrived) = refs[:-2], refs[-2:]
    width = squares.shape[1] // 2
    copies = [
        pieces(panels.at[0, 2 + step], held.at[step], arrived.at[step])
        for step in range(held.shape[0])
    ]
    both, high = operands(value[...])
    for step, out in enumerate(sent):
        tail_of(copies[step], held.at[step], both, high, width, out)
    with_squares(sent[-1], width, squares)


def more_tails(value, squares, panels, count):
    rows = value.shape[0]
    width = squares.shape[1] // 2
    shapes = [(width + 8 * (step == count - 1), rows) for step in range(count)]
    return pl.pallas_call(
        tails_kernel,
        out_shape=[shaped(*shape) for shape in shapes],
        in_specs=[VMEM, VMEM, HBM],
        out_specs=[VMEM] * count,
        scratch_shapes=[
            pltpu.VMEM((count, rows, rows), jnp.float32),
            pltpu.SemaphoreType.DMA((count, rows // PIECE)),
        ],
        cost_estimate=cost(1),
        compiler_params=limit(8 + 4 * count),
    )(value, squares, in_hbm(panels))


def last_kernel(leaves, count, where, own_rhs, halves, squares, got, first, second, kept, widths):
    left = left_of(own_rhs, (first, second))
    value = applied(halves[2], halves[3], *operands(doubled(left)))
    kept[...] = value
    total = (squares[...] + got[...]) + jnp.sum(value * value, axis=0, keepdims=True)
    value = jnp.sqrt(total / count + 1e-06)
    widths[...] = jnp.where(where[1] == leaves - 1, value, 0.0)


def last(leaves, count, where, own_rhs, halves, squares, got, parts):
    width, rows = own_rhs.shape
    return pl.pallas_call(
        functools.partial(last_kernel, leaves, count),
        out_shape=(shaped(rows, 2 * width), shaped(*squares.shape)),
        in_specs=[SMEM] + [VMEM] * 6,
        out_specs=(VMEM, VMEM),
        cost_estimate=cost(1),
        compiler_params=limit(8),
    )(where, own_rhs, in_vmem(halves), squares, got, *parts)


def settle_kernel(tiers, where, solved, value, out):
    width = out.shape[0]

    @pl.when(where[2] == tiers)
    def _():
        out[...] = value[...].T[:width]

    @pl.when(where[2] != tiers)
    def _():
        out[...] = solved[...]


def settled(tiers, where, solved, value):
    return pl.pallas_call(
        functools.partial(settle_kernel, tiers),
        out_shape=shaped(*solved.shape),
        in_specs=[SMEM, VMEM, VMEM],
        out_specs=VMEM,
        cost_estimate=cost(1),
        compiler_params=limit(6),
    )(where, solved, value)


def local(rhs_rows, order, leaf_inverse, leaf_panels, panel_mask, sep_rhs, sep_inverse, sep_panels):
    n_leaf = lax.axis_size("leaf")
    n_grid = lax.axis_size("grid")
    tiers = leaf_panels.shape[1]
    block_rows, columns = rhs_rows.shape
    block_count = n_leaf * n_grid
    sep_rows = sep_rhs.shape[1]
    width = columns // n_grid
    leaf = lax.axis_index("leaf").astype(jnp.int32)
    grid = lax.axis_index("grid").astype(jnp.int32)
    level = jnp.ones((), jnp.int32)
    for bit in range(1, tiers):
        level = level + ((leaf + 1) & (2**bit - 1) == 0).astype(jnp.int32)
    where = jnp.stack([grid, leaf, level])
    scale = jnp.repeat(panel_mask[0].astype(jnp.float32), 128, axis=1)

    picked = pick(rhs_rows, order)
    picked, where = lax.optimization_barrier((picked, where))
    moved = lax.all_to_all(
        picked.reshape(block_count, block_rows // block_count, columns),
        ("leaf", "grid"),
        split_axis=0,
        concat_axis=0,
        tiled=True,
    )
    permuted = moved.reshape(block_rows, columns)

    _, inverse, own_panels = lax.optimization_barrier((picked, sep_inverse, sep_panels))
    halves = prepared(inverse, own_panels)
    permuted, halves = lax.optimization_barrier((permuted, halves))

    given, kept = two_products(where, leaf_inverse, permuted, True)
    in_chip = lax.ppermute(given, "grid", [(0, 1), (1, 0), (2, 3)])
    onward = kept + in_chip
    onward, permuted, halves = lax.optimization_barrier((onward, permuted, halves))
    between = lax.ppermute(onward, "grid", [(0, 2), (1, 3)])
    *low_block, lowest = two_products(where, leaf_inverse, permuted, False)
    from_pair = [lax.ppermute(part, "grid", [(0, 1)]) for part in low_block]
    halves, panels = loaded(halves, leaf_panels)

    leaf_y, turned, squares, given, kept = first_update(
        where, (kept, in_chip, between, lowest, *low_block, *from_pair), scale, panels
    )
    swap = [(0, 1), (1, 0), (2, 3), (3, 2)]
    over = [(0, 2), (1, 3), (2, 0), (3, 1)]
    got = lax.ppermute(given, "grid", swap)
    given, other = second_update(where, turned, scale, panels)
    own, away = chip_sum(where, kept, got)
    away, given, turned = lax.optimization_barrier((away, given, turned))
    got = lax.ppermute(away, "grid", over)
    second, away = chip_sum(where, other, lax.ppermute(given, "grid", swap))
    given, kept = later_updates(where, squares, turned, scale, panels)
    got, away, given = lax.optimization_barrier((got, away, given))
    mine = own + got
    following = second + lax.ppermute(away, "grid", over)
    own, away = chip_sum(where, kept, lax.ppermute(given, "grid", swap))
    pairs = [(base + 1, base) for base in range(0, n_leaf, 2)]
    own, own_panels = lax.optimization_barrier((own, sep_panels))
    next_panel = loaded_panel(own_panels)
    got, own, next_panel = lax.optimization_barrier(
        (lax.ppermute(mine, "leaf", pairs), own, next_panel)
    )
    parts = [mine, got]
    edges = [(step * width, (step + 1) * width) for step in range(tiers - 2)]
    edges[-1] = (edges[-1][0], own.shape[0])
    rest = [
        own[start:stop] + lax.ppermute(away[start:stop], "grid", over) for start, stop in edges
    ]

    own_rhs = sep_rhs[0].T
    solved = jnp.zeros_like(own_rhs)
    waiting = []
    for tier in range(1, tiers):
        size = 2**tier
        direct_left, direct_right, early, onward, aside = [], [], [], [], []
        for base in range(0, n_leaf, size):
            host, end = (base + size // 2 - 1, base + size - 1)
            parent = base // (2 * size) * 2 * size + size - 1
            onward.append((host, end))
            if end == parent:
                direct_left.append((host, parent))
            else:
                direct_right.append((host, parent))
                early.append((end, parent))
                aside.append((host, end))
        left, term = direct(own_rhs, halves, parts)
        count = len(rest)
        solved, own, *more = solve(
            where, tier, left, halves, solved, next_panel if count else None, count == 1
        )
        if waiting:
            _, following, *waiting = lax.optimization_barrier((left, following, *waiting))
            rest = [
                other + lax.ppermute(other + tail, "leaf", before)
                for other, tail in zip(rest, waiting)
            ]
        if count:
            value, tail = more
            term = following + term
            from_left = lax.ppermute(term, "leaf", direct_left)
            if tier == 1:
                turn, tail = lax.optimization_barrier((lax.ppermute(term, "leaf", aside), tail))
                parts = [following, lax.ppermute(following + turn, "leaf", early), from_left]
            else:
                next_early = lax.ppermute(following, "leaf", early)
                from_right = lax.ppermute(term, "leaf", direct_right)
                parts = [following, next_early, from_left, from_right]
            following = rest[0] + lax.ppermute(rest[0] + tail, "leaf", onward)
            rest = rest[1:]
            waiting = []
            if count > 1:
                value, _ = lax.optimization_barrier((value, from_left))
                waiting = more_tails(value, own, sep_panels, count - 1)
                parts[1], *waiting = lax.optimization_barrier((parts[1], *waiting))
            before = onward
        else:
            squares = following[width:, : 2 * width]
            following = following[:width]
            parts = [following, lax.ppermute(following + term, "leaf", direct_left)]
            got = lax.ppermute(squares + own, "leaf", direct_left)
    value, widths = last(
        n_leaf,
        n_leaf * (block_rows * n_grid + sep_rows),
        where,
        own_rhs,
        halves,
        squares,
        got,
        parts,
    )
    solved = settled(tiers, where, solved, value)
    step = n_leaf
    while step > 1:
        half_step = step // 2
        steps = [(end, end - half_step) for end in range(step - 1, n_leaf, step)]
        widths = widths + lax.ppermute(widths, "leaf", steps)
        step = half_step
    return (leaf_y, solved.T[None], widths[0, :width])


def solution(mesh):
    placed = (
        P(("leaf", "grid"), None),
        P(("leaf", "grid")),
        P("leaf", "grid"),
        P("leaf", None, None, "grid"),
        P("leaf", None, "grid"),
        P("leaf", None, "grid"),
        P("leaf", None, None),
        P("leaf", None, None, None),
    )
    return jax.shard_map(
        local,
        mesh=mesh,
        in_specs=placed,
        out_specs=(P(("leaf", "grid"), None), P("leaf", None, "grid"), P("grid")),
        check_vma=False,
    )
```

```python
import functools

import jax
import jax.numpy as jnp
from jax import lax
from jax.experimental import pallas as pl
from jax.experimental.pallas import tpu as pltpu
from jax.sharding import PartitionSpec as P

HIGH = lax.Precision.HIGH
SMEM = pl.BlockSpec(memory_space=pltpu.SMEM)
VMEM = pl.BlockSpec(memory_space=pltpu.VMEM)
HBM = pl.BlockSpec(memory_space=pl.ANY)
PIECE = 128
MIB = 2**20


def shaped(*shape, dtype=jnp.float32):
    return jax.ShapeDtypeStruct(shape, dtype)


def cost(products):
    return pl.CostEstimate(flops=24 * products, bytes_accessed=4 * 2**20, transcendentals=0)


def limit(mebibytes):
    return pltpu.CompilerParams(vmem_limit_bytes=mebibytes * MIB)


def split(value):
    high = value.astype(jnp.bfloat16)
    return high, (value - high.astype(jnp.float32)).astype(jnp.bfloat16)


def split_wide(value):
    high = value.astype(jnp.bfloat16)
    return high, value - high.astype(jnp.float32)


def in_hbm(value):
    return pltpu.with_memory_space_constraint(value, pltpu.HBM)


def in_vmem(value):
    return pltpu.with_memory_space_constraint(value, pltpu.VMEM)


def pieces(source, held, arrived):
    copies = []
    for step in range(held.shape[0] // PIECE):
        at = pl.ds(step * PIECE, PIECE)
        copies.append(pltpu.make_async_copy(source.at[at], held.at[at], arrived.at[step]))
        copies[step].start()
    return copies


def wait(copies, rows):
    for copy in copies[rows.start // PIECE : rows.stop // PIECE]:
        copy.wait()


def whole(*shape):
    return pl.BlockSpec(shape, lambda *step: (0,) * len(shape))


def pick_kernel(order, rows, out):
    size = rows.shape[0]
    place = lax.broadcasted_iota(jnp.int32, (size, size), 0)
    chosen = jnp.where(place == order[...], 1.0, 0.0).T.astype(jnp.bfloat16)
    high, rest = split_wide(rows[...])
    middle, low = split(rest)
    value = jnp.dot(chosen, high, preferred_element_type=jnp.float32)
    value = value + jnp.dot(chosen, middle, preferred_element_type=jnp.float32)
    out[...] = value + jnp.dot(chosen, low, preferred_element_type=jnp.float32)


def pick(rows, order):
    size, columns = rows.shape
    return pl.pallas_call(
        pick_kernel,
        out_shape=shaped(size, columns),
        grid=(1,),
        in_specs=[whole(1, size), whole(size, columns)],
        out_specs=whole(size, columns),
        cost_estimate=cost(size * size * columns),
        compiler_params=limit(12),
    )(in_hbm(order.reshape(1, size)), in_hbm(rows))


def product_kernel(last_two, place, matrix, rows, *outs):
    size = rows.shape[0]
    for step in range(2):
        block = 2 + ((place[0] & 1) ^ (1 - step)) if last_two else 1 - step
        at = pl.ds(pl.multiple_of(block * size, size), size)
        value = jnp.dot(
            matrix[at], rows[...], precision=HIGH, preferred_element_type=jnp.float32
        )
        if last_two:
            outs[step][...] = value
        elif step == 0:
            outs[0][...] = value[: size // 2]
            outs[1][...] = value[size // 2 :]
        else:
            outs[2][...] = value


def two_products(place, matrix, rows, last_two):
    size, columns = rows.shape
    shapes = [size, size] if last_two else [size // 2, size // 2, size]
    return pl.pallas_call(
        functools.partial(product_kernel, last_two),
        out_shape=[shaped(count, columns) for count in shapes],
        in_specs=[SMEM, VMEM, VMEM],
        out_specs=[VMEM] * len(shapes),
        cost_estimate=cost(2 * size * size * columns),
        compiler_params=limit(8),
    )(place, in_vmem(matrix), rows)


def update_of(turned, scale, panel):
    return lax.dot_general(
        turned * scale,
        panel,
        (((1,), (1,)), ((), ())),
        precision=HIGH,
        preferred_element_type=jnp.float32,
    )


def hand_out(value, core, rows, lanes, width, given, kept):
    for mine in range(2):

        @pl.when(core == mine)
        def _(mine=mine):
            for half in range(2):
                at = (2 * half + mine) * width
                other = (2 * half + 1 - mine) * width
                kept[half, rows, lanes] = value[at : at + width]
                given[half, rows, lanes] = value[other : other + width]


def first_update_kernel(
    width, where, kept_in, in_chip, between, lowest, top, bottom, pair_top, pair_bottom, scale, panels,
    leaf_y, turned, squares, given, kept
):
    place = where[0]

    @pl.when(place == 0)
    def _():
        leaf_y[...] = lowest[...]

    @pl.when(place == 1)
    def _():
        middle = leaf_y.shape[0] // 2
        leaf_y[:middle] = top[...] + pair_top[...]
        leaf_y[middle:] = bottom[...] + pair_bottom[...]

    @pl.when(place == 2)
    def _():
        leaf_y[...] = kept_in[...] + between[...]

    @pl.when(place == 3)
    def _():
        leaf_y[...] = (kept_in[...] + in_chip[...]) + between[...]

    turned[...] = leaf_y[...].T
    value = update_of(turned[...], scale[0:1], panels[0])
    hand_out(value, place & 1, slice(None), slice(None), width, given, kept)
    own = jnp.sum(leaf_y[...] * leaf_y[...], axis=0, keepdims=True)
    squares[...] = jnp.broadcast_to(own, squares.shape)


def first_update(where, parts, scale, panels):
    size, columns = parts[0].shape
    rows = panels.shape[1]
    width = columns // 4
    halves = shaped(2, width, rows)
    return pl.pallas_call(
        functools.partial(first_update_kernel, width),
        out_shape=(
            shaped(size, columns), shaped(columns, size), shaped(8, columns), halves, halves
        ),
        in_specs=[SMEM] + [VMEM] * (len(parts) + 2),
        out_specs=(VMEM,) * 5,
        cost_estimate=cost(size * rows * columns),
        compiler_params=limit(12),
    )(where, *parts, scale, in_vmem(panels))


def second_update_kernel(width, where, turned, scale, panels, given, kept):
    every = slice(None)
    value = update_of(turned[...], scale[1:2], panels[1])
    hand_out(value, where[0] & 1, every, every, width, given, kept)


def second_update(where, turned, scale, panels):
    columns, size = turned.shape
    rows = panels.shape[1]
    width = columns // 4
    halves = shaped(2, width, rows)
    return pl.pallas_call(
        functools.partial(second_update_kernel, width),
        out_shape=(halves, halves),
        in_specs=[SMEM] + [VMEM] * 3,
        out_specs=(VMEM, VMEM),
        cost_estimate=cost(size * rows * columns),
        compiler_params=limit(8),
    )(where, turned, scale, in_vmem(panels))


def later_update_kernel(width, where, squares, turned, scale, panels, given, kept):
    core = where[0] & 1
    tiers = panels.shape[0]
    for tier in range(2, tiers):
        value = update_of(turned[...], scale[tier : tier + 1], panels[tier])
        rows = slice((tier - 2) * width, (tier - 1) * width)
        hand_out(value, core, rows, slice(None), width, given, kept)
    at = (tiers - 2) * width
    for refs, of in ((given, 1 - core), (kept, core)):
        refs[:, at:, :] = jnp.zeros((2, 8, refs.shape[2]), jnp.float32)
        for half in range(2):
            pair = squares[:, 2 * width * half : 2 * width * (half + 1)]
            pair = jnp.where(of == 0, pair, pltpu.roll(pair, width, 1))
            refs[half, at:, 0 : 2 * width] = pair


def later_updates(where, squares, turned, scale, panels):
    columns, size = turned.shape
    tiers, rows = panels.shape[:2]
    width = columns // 4
    halves = shaped(2, (tiers - 2) * width + 8, rows)
    return pl.pallas_call(
        functools.partial(later_update_kernel, width),
        out_shape=(halves, halves),
        in_specs=[SMEM] + [VMEM] * 4,
        out_specs=(VMEM, VMEM),
        cost_estimate=cost(1),
        compiler_params=limit(12),
    )(where, squares, turned, scale, in_vmem(panels))


def chip_sum_kernel(where, kept, got, own, away):
    half = where[0] >> 1
    own[...] = kept[half] + got[half]
    away[...] = kept[1 - half] + got[1 - half]


def chip_sum(where, kept, got):
    shape = shaped(*kept.shape[1:])
    return pl.pallas_call(
        chip_sum_kernel,
        out_shape=(shape, shape),
        in_specs=[SMEM, VMEM, VMEM],
        out_specs=(VMEM, VMEM),
        cost_estimate=cost(1),
        compiler_params=limit(6),
    )(where, kept, got)


def prepare_kernel(
    inverse, panels, out, wide, direct_high, direct_low, high, low, inverse_arrived, panel_arrived, gone
):
    rows = high.shape[0]
    block = rows // 4
    copies = pieces(inverse.at[0], wide.at[0], inverse_arrived)
    pieces(panels.at[0, 0], wide.at[1], panel_arrived)
    for at in range(0, rows, block):
        part = slice(at, at + block)
        wait(copies, part)
        high[part], low[part] = split(wide[0, part])
    sent = [
        pltpu.make_async_copy(source, out.at[2 + step], gone.at[step])
        for step, source in enumerate((high, low))
    ]
    for copy in sent:
        copy.start()

    def part_sent(step):
        part = pl.ds(pl.multiple_of(step * block, block), block)
        return [
            pltpu.make_async_copy(source.at[part], out.at[which, part], gone.at[2 + which])
            for which, source in enumerate((direct_high, direct_low))
        ]

    @pl.loop(0, 4)
    def _(step):
        part = pl.ds(pl.multiple_of(step * block, block), block)
        for piece in range(block // PIECE):
            at = pl.ds(pl.multiple_of(step * block + piece * PIECE, PIECE), PIECE)
            pltpu.make_async_copy(
                panels.at[0, 0, at], wide.at[1, at], panel_arrived.at[step * (block // PIECE) + piece]
            ).wait()
        panel_high, panel_low = split(wide[1, part])
        for at in range(0, rows, block):
            lanes = slice(at, at + block)
            both = high[at:, lanes]
            value = jnp.dot(panel_high[:, at:], both, preferred_element_type=jnp.float32)
            value = value + jnp.dot(panel_low[:, at:], both, preferred_element_type=jnp.float32)
            value = value + jnp.dot(
                panel_high[:, at:], low[at:, lanes], preferred_element_type=jnp.float32
            )
            direct_high[part, lanes], direct_low[part, lanes] = split(value)

        @pl.when(step > 0)
        def _():
            for copy in part_sent(step - 1):
                copy.wait()

        for copy in part_sent(step):
            copy.start()

    for copy in sent + part_sent(3):
        copy.wait()


def prepared(sep_inverse, sep_panels):
    rows = sep_inverse.shape[1]
    return pl.pallas_call(
        prepare_kernel,
        out_shape=pltpu.HBM((4, rows, rows), jnp.bfloat16),
        in_specs=[HBM] * 2,
        out_specs=HBM,
        scratch_shapes=[pltpu.VMEM((2, rows, rows), jnp.float32)]
        + [pltpu.VMEM((rows, rows), jnp.bfloat16)] * 4
        + [
            pltpu.SemaphoreType.DMA((rows // PIECE,)),
            pltpu.SemaphoreType.DMA((rows // PIECE,)),
            pltpu.SemaphoreType.DMA((4,)),
        ],
        cost_estimate=cost(rows**3),
        compiler_params=limit(24),
    )(in_hbm(sep_inverse), in_hbm(sep_panels))


def load_kernel(halves, panels, halves_out, panels_out, arrived):
    copies = [(panels.at[0, step], panels_out.at[step]) for step in range(panels_out.shape[0])]
    copies += [(halves.at[step], halves_out.at[step]) for step in range(4)]
    copies = [
        pltpu.make_async_copy(source, target, arrived.at[step])
        for step, (source, target) in enumerate(copies)
    ]
    for copy in copies:
        copy.start()
    for copy in copies:
        copy.wait()


def loaded(halves, leaf_panels):
    return pl.pallas_call(
        load_kernel,
        out_shape=(
            pltpu.VMEM(halves.shape, jnp.bfloat16),
            pltpu.VMEM(leaf_panels.shape[1:], jnp.float32),
        ),
        in_specs=[HBM] * 2,
        out_specs=(VMEM,) * 2,
        scratch_shapes=[pltpu.SemaphoreType.DMA((4 + leaf_panels.shape[1],))],
        cost_estimate=cost(1),
        compiler_params=limit(4),
    )(in_hbm(halves), in_hbm(leaf_panels))


def load_panel_kernel(panels, out, arrived):
    copies = pieces(panels.at[0, 1], out, arrived)
    wait(copies, slice(0, out.shape[0]))


def loaded_panel(panels):
    rows = panels.shape[2]
    return pl.pallas_call(
        load_panel_kernel,
        out_shape=pltpu.VMEM(panels.shape[2:], jnp.float32),
        in_specs=[HBM],
        out_specs=VMEM,
        scratch_shapes=[pltpu.SemaphoreType.DMA((rows // PIECE,))],
        cost_estimate=cost(1),
        compiler_params=limit(4),
    )(in_hbm(panels))


def operands(value):
    width = value.shape[1] // 2
    lane = lax.broadcasted_iota(jnp.int32, value.shape, 1)
    high = value.astype(jnp.bfloat16)
    as_wide = high.astype(jnp.float32)
    return jnp.where(lane < width, as_wide, value - as_wide).astype(jnp.bfloat16), high


def applied(matrix_high, matrix_low, both, high):
    first = jnp.dot(matrix_high, both, preferred_element_type=jnp.float32)
    second = jnp.dot(matrix_low, high, preferred_element_type=jnp.float32)
    return (first + pltpu.roll(first, first.shape[1] // 2, 1)) + second


def doubled(value):
    return jnp.concatenate([value, value], axis=0).T


def left_of(own_rhs, parts):
    total = parts[0][...]
    for part in parts[1:]:
        total = total + part[...]
    return own_rhs[...] - total


def direct_kernel(tier, count, where, own_rhs, halves, *refs):
    parts, (left, term) = refs[:count], refs[count:]

    @pl.when(where[2] == tier)
    def _():
        left[...] = left_of(own_rhs, parts)
        value = applied(halves[0], halves[1], *operands(doubled(left[...])))
        term[...] = value.T[: term.shape[0]]


def direct(where, tier, own_rhs, halves, parts):
    width, rows = own_rhs.shape
    return pl.pallas_call(
        functools.partial(direct_kernel, tier, len(parts)),
        out_shape=(shaped(width, rows), shaped(width, rows)),
        in_specs=[SMEM] + [VMEM] * (2 + len(parts)),
        out_specs=(VMEM, VMEM),
        cost_estimate=cost(rows**2 * 64),
        compiler_params=limit(8),
    )(where, own_rhs, in_vmem(halves), *parts)


def tail_of(copies, held, both, high, width, out):
    rows = held.shape[0]
    block = rows // 4
    for at in range(0, rows, block):
        part = slice(at, at + block)
        if copies:
            wait(copies, part)
        out[:width, part] = applied(*split(held[part]), both, high).T[:width]


def with_squares(out, width, squares):
    out[width:, :] = jnp.zeros((8, out.shape[1]), jnp.float32)
    out[width:, : squares.shape[1]] = squares[...]


def solve_kernel(tier, last, with_tail, where, left, halves, solved, *refs):
    panel, refs = refs[0] if with_tail else None, refs[with_tail:]
    out, squares, kept, *sent = refs
    width = left.shape[0]

    @pl.when(where[2] != tier)
    def _():
        out[...] = solved[...]

    @pl.when(where[2] == tier)
    def _():
        value = applied(halves[2], halves[3], *operands(doubled(left[...])))
        out[...] = value.T[:width]
        kept[...] = value
        own = jnp.sum(value * value, axis=0, keepdims=True)
        squares[...] = jnp.broadcast_to(own, squares.shape)
        if sent:
            tail_of(None, panel, *operands(value), width, sent[0])
            if last:
                with_squares(sent[0], width, squares)


def solve(where, tier, left, halves, solved, panel=None, last=False):
    width, rows = left.shape
    with_tail = panel is not None
    return pl.pallas_call(
        functools.partial(solve_kernel, tier, last, with_tail),
        out_shape=[shaped(width, rows), shaped(8, 2 * width), shaped(rows, 2 * width)]
        + [shaped(width + 8 * last, rows)] * with_tail,
        in_specs=[SMEM] + [VMEM] * (3 + with_tail),
        out_specs=[VMEM] * (3 + with_tail),
        cost_estimate=cost(1),
        compiler_params=limit(8),
    )(where, left, in_vmem(halves), solved, *([in_vmem(panel)] if with_tail else []))


def tails_kernel(tier, where, value, squares, panels, *refs):
    sent, (held, arrived) = refs[:-2], refs[-2:]
    width = squares.shape[1] // 2

    @pl.when(where[2] == tier)
    def _():
        copies = [
            pieces(panels.at[0, 2 + step], held.at[step], arrived.at[step])
            for step in range(held.shape[0])
        ]
        both, high = operands(value[...])
        for step, out in enumerate(sent):
            tail_of(copies[step], held.at[step], both, high, width, out)
        with_squares(sent[-1], width, squares)


def more_tails(where, tier, value, squares, panels, count):
    rows = value.shape[0]
    width = squares.shape[1] // 2
    shapes = [(width + 8 * (step == count - 1), rows) for step in range(count)]
    return pl.pallas_call(
        functools.partial(tails_kernel, tier),
        out_shape=[shaped(*shape) for shape in shapes],
        in_specs=[SMEM, VMEM, VMEM, HBM],
        out_specs=[VMEM] * count,
        scratch_shapes=[
            pltpu.VMEM((count, rows, rows), jnp.float32),
            pltpu.SemaphoreType.DMA((count, rows // PIECE)),
        ],
        cost_estimate=cost(1),
        compiler_params=limit(8 + 4 * count),
    )(where, value, squares, in_hbm(panels))


def last_kernel(leaves, count, where, own_rhs, halves, squares, got, first, second, kept, widths):

    @pl.when(where[1] != leaves - 1)
    def _():
        widths[...] = jnp.zeros_like(widths)

    @pl.when(where[1] == leaves - 1)
    def _():
        left = left_of(own_rhs, (first, second))
        value = applied(halves[2], halves[3], *operands(doubled(left)))
        kept[...] = value
        total = (squares[...] + got[...]) + jnp.sum(value * value, axis=0, keepdims=True)
        widths[...] = jnp.sqrt(total / count + 1e-06)


def last(leaves, count, where, own_rhs, halves, squares, got, parts):
    width, rows = own_rhs.shape
    return pl.pallas_call(
        functools.partial(last_kernel, leaves, count),
        out_shape=(shaped(rows, 2 * width), shaped(*squares.shape)),
        in_specs=[SMEM] + [VMEM] * 6,
        out_specs=(VMEM, VMEM),
        cost_estimate=cost(1),
        compiler_params=limit(8),
    )(where, own_rhs, in_vmem(halves), squares, got, *parts)


def settle_kernel(tiers, where, solved, value, out):
    width = out.shape[0]

    @pl.when(where[2] == tiers)
    def _():
        out[...] = value[...].T[:width]

    @pl.when(where[2] != tiers)
    def _():
        out[...] = solved[...]


def settled(tiers, where, solved, value):
    return pl.pallas_call(
        functools.partial(settle_kernel, tiers),
        out_shape=shaped(*solved.shape),
        in_specs=[SMEM, VMEM, VMEM],
        out_specs=VMEM,
        cost_estimate=cost(1),
        compiler_params=limit(6),
    )(where, solved, value)


def local(rhs_rows, order, leaf_inverse, leaf_panels, panel_mask, sep_rhs, sep_inverse, sep_panels):
    n_leaf = lax.axis_size("leaf")
    n_grid = lax.axis_size("grid")
    tiers = leaf_panels.shape[1]
    block_rows, columns = rhs_rows.shape
    block_count = n_leaf * n_grid
    sep_rows = sep_rhs.shape[1]
    width = columns // n_grid
    leaf = lax.axis_index("leaf").astype(jnp.int32)
    grid = lax.axis_index("grid").astype(jnp.int32)
    level = jnp.ones((), jnp.int32)
    for bit in range(1, tiers):
        level = level + ((leaf + 1) & (2**bit - 1) == 0).astype(jnp.int32)
    where = jnp.stack([grid, leaf, level])
    scale = jnp.repeat(panel_mask[0].astype(jnp.float32), 128, axis=1)

    picked = pick(rhs_rows, order)
    picked, where = lax.optimization_barrier((picked, where))
    moved = lax.all_to_all(
        picked.reshape(block_count, block_rows // block_count, columns),
        ("leaf", "grid"),
        split_axis=0,
        concat_axis=0,
        tiled=True,
    )
    permuted = moved.reshape(block_rows, columns)

    _, inverse, own_panels = lax.optimization_barrier((picked, sep_inverse, sep_panels))
    halves = prepared(inverse, own_panels)
    permuted, halves = lax.optimization_barrier((permuted, halves))

    given, kept = two_products(where, leaf_inverse, permuted, True)
    in_chip = lax.ppermute(given, "grid", [(0, 1), (1, 0), (2, 3)])
    onward = kept + in_chip
    onward, permuted, halves = lax.optimization_barrier((onward, permuted, halves))
    between = lax.ppermute(onward, "grid", [(0, 2), (1, 3)])
    *low_block, lowest = two_products(where, leaf_inverse, permuted, False)
    from_pair = [lax.ppermute(part, "grid", [(0, 1)]) for part in low_block]
    halves, panels = loaded(halves, leaf_panels)

    leaf_y, turned, squares, given, kept = first_update(
        where, (kept, in_chip, between, lowest, *low_block, *from_pair), scale, panels
    )
    swap = [(0, 1), (1, 0), (2, 3), (3, 2)]
    over = [(0, 2), (1, 3), (2, 0), (3, 1)]
    got = lax.ppermute(given, "grid", swap)
    given, other = second_update(where, turned, scale, panels)
    own, away = chip_sum(where, kept, got)
    away, given, turned = lax.optimization_barrier((away, given, turned))
    got = lax.ppermute(away, "grid", over)
    second, away = chip_sum(where, other, lax.ppermute(given, "grid", swap))
    given, kept = later_updates(where, squares, turned, scale, panels)
    got, away, given = lax.optimization_barrier((got, away, given))
    mine = own + got
    following = second + lax.ppermute(away, "grid", over)
    own, away = chip_sum(where, kept, lax.ppermute(given, "grid", swap))
    pairs = [(base + 1, base) for base in range(0, n_leaf, 2)]
    own, own_panels = lax.optimization_barrier((own, sep_panels))
    next_panel = loaded_panel(own_panels)
    got, own, next_panel = lax.optimization_barrier(
        (lax.ppermute(mine, "leaf", pairs), own, next_panel)
    )
    parts = [mine, got]
    edges = [(step * width, (step + 1) * width) for step in range(tiers - 2)]
    edges[-1] = (edges[-1][0], own.shape[0])
    rest = [
        own[start:stop] + lax.ppermute(away[start:stop], "grid", over) for start, stop in edges
    ]

    own_rhs = sep_rhs[0].T
    solved = jnp.zeros_like(own_rhs)
    waiting = []
    for tier in range(1, tiers):
        size = 2**tier
        direct_left, direct_right, early, onward, aside = [], [], [], [], []
        for base in range(0, n_leaf, size):
            host, end = (base + size // 2 - 1, base + size - 1)
            parent = base // (2 * size) * 2 * size + size - 1
            onward.append((host, end))
            if end == parent:
                direct_left.append((host, parent))
            else:
                direct_right.append((host, parent))
                early.append((end, parent))
                aside.append((host, end))
        left, term = direct(where, tier, own_rhs, halves, parts)
        count = len(rest)
        solved, own, *more = solve(
            where, tier, left, halves, solved, next_panel if count else None, count == 1
        )
        if waiting:
            _, following, *waiting = lax.optimization_barrier((left, following, *waiting))
            rest = [
                other + lax.ppermute(other + tail, "leaf", before)
                for other, tail in zip(rest, waiting)
            ]
        if count:
            value, tail = more
            if tier > 1:
                term, tail = lax.optimization_barrier((term, tail))
            term = following + term
            from_left = lax.ppermute(term, "leaf", direct_left)
            if tier == 1:
                turn, tail = lax.optimization_barrier((lax.ppermute(term, "leaf", aside), tail))
                parts = [following, lax.ppermute(following + turn, "leaf", early), from_left]
            else:
                next_early = lax.ppermute(following, "leaf", early)
                from_right = lax.ppermute(term, "leaf", direct_right)
                parts = [following, next_early, from_left, from_right]
            following = rest[0] + lax.ppermute(rest[0] + tail, "leaf", onward)
            rest = rest[1:]
            waiting = []
            if count > 1:
                value, _ = lax.optimization_barrier((value, from_left))
                waiting = more_tails(where, tier, value, own, sep_panels, count - 1)
                parts[1], *waiting = lax.optimization_barrier((parts[1], *waiting))
            before = onward
        else:
            squares = following[width:, : 2 * width]
            following = following[:width]
            parts = [following, lax.ppermute(following + term, "leaf", direct_left)]
            got = lax.ppermute(squares + own, "leaf", direct_left)
    value, widths = last(
        n_leaf,
        n_leaf * (block_rows * n_grid + sep_rows),
        where,
        own_rhs,
        halves,
        squares,
        got,
        parts,
    )
    solved = settled(tiers, where, solved, value)
    step = n_leaf
    while step > 1:
        half_step = step // 2
        steps = [(end, end - half_step) for end in range(step - 1, n_leaf, step)]
        widths = widths + lax.ppermute(widths, "leaf", steps)
        step = half_step
    return (leaf_y, solved.T[None], widths[0, :width])


def solution(mesh):
    placed = (
        P(("leaf", "grid"), None),
        P(("leaf", "grid")),
        P("leaf", "grid"),
        P("leaf", None, None, "grid"),
        P("leaf", None, "grid"),
        P("leaf", None, "grid"),
        P("leaf", None, None),
        P("leaf", None, None, None),
    )
    return jax.shard_map(
        local,
        mesh=mesh,
        in_specs=placed,
        out_specs=(P(("leaf", "grid"), None), P("leaf", None, "grid"), P("grid")),
        check_vma=False,
    )
```

```python
import functools

import jax
import jax.numpy as jnp
from jax import lax
from jax.experimental import pallas as pl
from jax.experimental.pallas import tpu as pltpu
from jax.sharding import PartitionSpec as P

HIGH = lax.Precision.HIGH
SMEM = pl.BlockSpec(memory_space=pltpu.SMEM)
VMEM = pl.BlockSpec(memory_space=pltpu.VMEM)
HBM = pl.BlockSpec(memory_space=pl.ANY)
PIECE = 128
MIB = 2**20


def shaped(*shape, dtype=jnp.float32):
    return jax.ShapeDtypeStruct(shape, dtype)


def cost(products):
    return pl.CostEstimate(flops=24 * products, bytes_accessed=4 * 2**20, transcendentals=0)


def limit(mebibytes):
    return pltpu.CompilerParams(vmem_limit_bytes=mebibytes * MIB)


def split(value):
    high = value.astype(jnp.bfloat16)
    return high, (value - high.astype(jnp.float32)).astype(jnp.bfloat16)


def split_wide(value):
    high = value.astype(jnp.bfloat16)
    return high, value - high.astype(jnp.float32)


def in_hbm(value):
    return pltpu.with_memory_space_constraint(value, pltpu.HBM)


def in_vmem(value):
    return pltpu.with_memory_space_constraint(value, pltpu.VMEM)


def pieces(source, held, arrived):
    copies = []
    for step in range(held.shape[0] // PIECE):
        at = pl.ds(step * PIECE, PIECE)
        copies.append(pltpu.make_async_copy(source.at[at], held.at[at], arrived.at[step]))
        copies[step].start()
    return copies


def wait(copies, rows):
    for copy in copies[rows.start // PIECE : rows.stop // PIECE]:
        copy.wait()


def whole(*shape):
    return pl.BlockSpec(shape, lambda *step: (0,) * len(shape))


def pick_kernel(order, rows, out):
    size = rows.shape[0]
    place = lax.broadcasted_iota(jnp.int32, (size, size), 0)
    chosen = jnp.where(place == order[...], 1.0, 0.0).T.astype(jnp.bfloat16)
    high, rest = split_wide(rows[...])
    middle, low = split(rest)
    value = jnp.dot(chosen, high, preferred_element_type=jnp.float32)
    value = value + jnp.dot(chosen, middle, preferred_element_type=jnp.float32)
    out[...] = value + jnp.dot(chosen, low, preferred_element_type=jnp.float32)


def pick(rows, order):
    size, columns = rows.shape
    return pl.pallas_call(
        pick_kernel,
        out_shape=shaped(size, columns),
        grid=(1,),
        in_specs=[whole(1, size), whole(size, columns)],
        out_specs=whole(size, columns),
        cost_estimate=cost(size * size * columns),
        compiler_params=limit(12),
    )(in_hbm(order.reshape(1, size)), in_hbm(rows))


def product_kernel(last_two, place, matrix, rows, *outs):
    size = rows.shape[0]
    for step in range(2):
        block = 2 + ((place[0] & 1) ^ (1 - step)) if last_two else 1 - step
        at = pl.ds(pl.multiple_of(block * size, size), size)
        value = jnp.dot(
            matrix[at], rows[...], precision=HIGH, preferred_element_type=jnp.float32
        )
        if last_two:
            outs[step][...] = value
        elif step == 0:
            outs[0][...] = value[: size // 2]
            outs[1][...] = value[size // 2 :]
        else:
            outs[2][...] = value


def two_products(place, matrix, rows, last_two):
    size, columns = rows.shape
    shapes = [size, size] if last_two else [size // 2, size // 2, size]
    return pl.pallas_call(
        functools.partial(product_kernel, last_two),
        out_shape=[shaped(count, columns) for count in shapes],
        in_specs=[SMEM, VMEM, VMEM],
        out_specs=[VMEM] * len(shapes),
        cost_estimate=cost(2 * size * size * columns),
        compiler_params=limit(8),
    )(place, in_vmem(matrix), rows)


def update_of(turned, scale, panel):
    return lax.dot_general(
        turned * scale,
        panel,
        (((1,), (1,)), ((), ())),
        precision=HIGH,
        preferred_element_type=jnp.float32,
    )


def hand_out(value, core, rows, lanes, width, given, kept):
    for mine in range(2):

        @pl.when(core == mine)
        def _(mine=mine):
            for half in range(2):
                at = (2 * half + mine) * width
                other = (2 * half + 1 - mine) * width
                kept[half, rows, lanes] = value[at : at + width]
                given[half, rows, lanes] = value[other : other + width]


def first_update_kernel(
    width, where, kept_in, in_chip, between, lowest, top, bottom, pair_top, pair_bottom, scale, panels,
    leaf_y, turned, squares, given, kept
):
    place = where[0]

    @pl.when(place == 0)
    def _():
        leaf_y[...] = lowest[...]

    @pl.when(place == 1)
    def _():
        middle = leaf_y.shape[0] // 2
        leaf_y[:middle] = top[...] + pair_top[...]
        leaf_y[middle:] = bottom[...] + pair_bottom[...]

    @pl.when(place == 2)
    def _():
        leaf_y[...] = kept_in[...] + between[...]

    @pl.when(place == 3)
    def _():
        leaf_y[...] = (kept_in[...] + in_chip[...]) + between[...]

    turned[...] = leaf_y[...].T
    value = update_of(turned[...], scale[0:1], panels[0])
    hand_out(value, place & 1, slice(None), slice(None), width, given, kept)
    own = jnp.sum(leaf_y[...] * leaf_y[...], axis=0, keepdims=True)
    squares[...] = jnp.broadcast_to(own, squares.shape)


def first_update(where, parts, scale, panels):
    size, columns = parts[0].shape
    rows = panels.shape[1]
    width = columns // 4
    halves = shaped(2, width, rows)
    return pl.pallas_call(
        functools.partial(first_update_kernel, width),
        out_shape=(
            shaped(size, columns), shaped(columns, size), shaped(8, columns), halves, halves
        ),
        in_specs=[SMEM] + [VMEM] * (len(parts) + 2),
        out_specs=(VMEM,) * 5,
        cost_estimate=cost(size * rows * columns),
        compiler_params=limit(12),
    )(where, *parts, scale, in_vmem(panels))


def second_update_kernel(width, where, turned, scale, panels, given, kept):
    every = slice(None)
    value = update_of(turned[...], scale[1:2], panels[1])
    hand_out(value, where[0] & 1, every, every, width, given, kept)


def second_update(where, turned, scale, panels):
    columns, size = turned.shape
    rows = panels.shape[1]
    width = columns // 4
    halves = shaped(2, width, rows)
    return pl.pallas_call(
        functools.partial(second_update_kernel, width),
        out_shape=(halves, halves),
        in_specs=[SMEM] + [VMEM] * 3,
        out_specs=(VMEM, VMEM),
        cost_estimate=cost(size * rows * columns),
        compiler_params=limit(8),
    )(where, turned, scale, in_vmem(panels))


def later_update_kernel(width, where, squares, turned, scale, panels, given, kept):
    core = where[0] & 1
    tiers = panels.shape[0]
    for tier in range(2, tiers):
        value = update_of(turned[...], scale[tier : tier + 1], panels[tier])
        rows = slice((tier - 2) * width, (tier - 1) * width)
        hand_out(value, core, rows, slice(None), width, given, kept)
    at = (tiers - 2) * width
    for refs, of in ((given, 1 - core), (kept, core)):
        refs[:, at:, :] = jnp.zeros((2, 8, refs.shape[2]), jnp.float32)
        for half in range(2):
            pair = squares[:, 2 * width * half : 2 * width * (half + 1)]
            pair = jnp.where(of == 0, pair, pltpu.roll(pair, width, 1))
            refs[half, at:, 0 : 2 * width] = pair


def later_updates(where, squares, turned, scale, panels):
    columns, size = turned.shape
    tiers, rows = panels.shape[:2]
    width = columns // 4
    halves = shaped(2, (tiers - 2) * width + 8, rows)
    return pl.pallas_call(
        functools.partial(later_update_kernel, width),
        out_shape=(halves, halves),
        in_specs=[SMEM] + [VMEM] * 4,
        out_specs=(VMEM, VMEM),
        cost_estimate=cost(1),
        compiler_params=limit(12),
    )(where, squares, turned, scale, in_vmem(panels))


def chip_sum_kernel(where, kept, got, own, away):
    half = where[0] >> 1
    own[...] = kept[half] + got[half]
    away[...] = kept[1 - half] + got[1 - half]


def chip_sum(where, kept, got):
    shape = shaped(*kept.shape[1:])
    return pl.pallas_call(
        chip_sum_kernel,
        out_shape=(shape, shape),
        in_specs=[SMEM, VMEM, VMEM],
        out_specs=(VMEM, VMEM),
        cost_estimate=cost(1),
        compiler_params=limit(6),
    )(where, kept, got)


def prepare_kernel(
    inverse, panels, out, wide, direct_high, direct_low, high, low, inverse_arrived, panel_arrived, gone
):
    rows = high.shape[0]
    block = rows // 4
    copies = pieces(inverse.at[0], wide.at[0], inverse_arrived)
    pieces(panels.at[0, 0], wide.at[1], panel_arrived)
    for at in range(0, rows, block):
        part = slice(at, at + block)
        wait(copies, part)
        high[part], low[part] = split(wide[0, part])
    sent = [
        pltpu.make_async_copy(source, out.at[2 + step], gone.at[step])
        for step, source in enumerate((high, low))
    ]
    for copy in sent:
        copy.start()

    def part_sent(step):
        part = pl.ds(pl.multiple_of(step * block, block), block)
        return [
            pltpu.make_async_copy(source.at[part], out.at[which, part], gone.at[2 + which])
            for which, source in enumerate((direct_high, direct_low))
        ]

    @pl.loop(0, 4)
    def _(step):
        part = pl.ds(pl.multiple_of(step * block, block), block)
        for piece in range(block // PIECE):
            at = pl.ds(pl.multiple_of(step * block + piece * PIECE, PIECE), PIECE)
            pltpu.make_async_copy(
                panels.at[0, 0, at], wide.at[1, at], panel_arrived.at[step * (block // PIECE) + piece]
            ).wait()
        panel_high, panel_low = split(wide[1, part])
        for at in range(0, rows, block):
            lanes = slice(at, at + block)
            both = high[at:, lanes]
            value = jnp.dot(panel_high[:, at:], both, preferred_element_type=jnp.float32)
            value = value + jnp.dot(panel_low[:, at:], both, preferred_element_type=jnp.float32)
            value = value + jnp.dot(
                panel_high[:, at:], low[at:, lanes], preferred_element_type=jnp.float32
            )
            direct_high[part, lanes], direct_low[part, lanes] = split(value)

        @pl.when(step > 0)
        def _():
            for copy in part_sent(step - 1):
                copy.wait()

        for copy in part_sent(step):
            copy.start()

    for copy in sent + part_sent(3):
        copy.wait()


def prepared(sep_inverse, sep_panels):
    rows = sep_inverse.shape[1]
    return pl.pallas_call(
        prepare_kernel,
        out_shape=pltpu.HBM((4, rows, rows), jnp.bfloat16),
        in_specs=[HBM] * 2,
        out_specs=HBM,
        scratch_shapes=[pltpu.VMEM((2, rows, rows), jnp.float32)]
        + [pltpu.VMEM((rows, rows), jnp.bfloat16)] * 4
        + [
            pltpu.SemaphoreType.DMA((rows // PIECE,)),
            pltpu.SemaphoreType.DMA((rows // PIECE,)),
            pltpu.SemaphoreType.DMA((4,)),
        ],
        cost_estimate=cost(rows**3),
        compiler_params=limit(24),
    )(in_hbm(sep_inverse), in_hbm(sep_panels))


def load_kernel(halves, panels, halves_out, panels_out, arrived):
    copies = [(panels.at[0, step], panels_out.at[step]) for step in range(panels_out.shape[0])]
    copies += [(halves.at[step], halves_out.at[step]) for step in range(4)]
    copies = [
        pltpu.make_async_copy(source, target, arrived.at[step])
        for step, (source, target) in enumerate(copies)
    ]
    for copy in copies:
        copy.start()
    for copy in copies:
        copy.wait()


def loaded(halves, leaf_panels):
    return pl.pallas_call(
        load_kernel,
        out_shape=(
            pltpu.VMEM(halves.shape, jnp.bfloat16),
            pltpu.VMEM(leaf_panels.shape[1:], jnp.float32),
        ),
        in_specs=[HBM] * 2,
        out_specs=(VMEM,) * 2,
        scratch_shapes=[pltpu.SemaphoreType.DMA((4 + leaf_panels.shape[1],))],
        cost_estimate=cost(1),
        compiler_params=limit(4),
    )(in_hbm(halves), in_hbm(leaf_panels))


def load_panel_kernel(panels, out, arrived):
    copies = pieces(panels.at[0, 1], out, arrived)
    wait(copies, slice(0, out.shape[0]))


def loaded_panel(panels):
    rows = panels.shape[2]
    return pl.pallas_call(
        load_panel_kernel,
        out_shape=pltpu.VMEM(panels.shape[2:], jnp.float32),
        in_specs=[HBM],
        out_specs=VMEM,
        scratch_shapes=[pltpu.SemaphoreType.DMA((rows // PIECE,))],
        cost_estimate=cost(1),
        compiler_params=limit(4),
    )(in_hbm(panels))


def operands(value):
    width = value.shape[1] // 2
    lane = lax.broadcasted_iota(jnp.int32, value.shape, 1)
    high = value.astype(jnp.bfloat16)
    as_wide = high.astype(jnp.float32)
    return jnp.where(lane < width, as_wide, value - as_wide).astype(jnp.bfloat16), high


def applied(matrix_high, matrix_low, both, high):
    first = jnp.dot(matrix_high, both, preferred_element_type=jnp.float32)
    second = jnp.dot(matrix_low, high, preferred_element_type=jnp.float32)
    return (first + pltpu.roll(first, first.shape[1] // 2, 1)) + second


def doubled(value):
    return jnp.concatenate([value, value], axis=0).T


def left_of(own_rhs, parts):
    total = parts[0][...]
    for part in parts[1:]:
        total = total + part[...]
    return own_rhs[...] - total


def direct_kernel(tier, count, where, own_rhs, halves, *refs):
    parts, (left, term) = refs[:count], refs[count:]

    @pl.when(where[2] == tier)
    def _():
        left[...] = left_of(own_rhs, parts)
        value = applied(halves[0], halves[1], *operands(doubled(left[...])))
        term[...] = value.T[: term.shape[0]]


def direct(where, tier, own_rhs, halves, parts):
    width, rows = own_rhs.shape
    return pl.pallas_call(
        functools.partial(direct_kernel, tier, len(parts)),
        out_shape=(shaped(width, rows), shaped(width, rows)),
        in_specs=[SMEM] + [VMEM] * (2 + len(parts)),
        out_specs=(VMEM, VMEM),
        cost_estimate=cost(rows**2 * 64),
        compiler_params=limit(8),
    )(where, own_rhs, in_vmem(halves), *parts)


def tail_of(copies, held, both, high, width, out):
    rows = held.shape[0]
    block = rows // 4
    for at in range(0, rows, block):
        part = slice(at, at + block)
        if copies:
            wait(copies, part)
        out[:width, part] = applied(*split(held[part]), both, high).T[:width]


def with_squares(out, width, squares):
    out[width:, :] = jnp.zeros((8, out.shape[1]), jnp.float32)
    out[width:, : squares.shape[1]] = squares[...]


def solve_kernel(tier, last, with_tail, where, left, halves, solved, *refs):
    panel, refs = refs[0] if with_tail else None, refs[with_tail:]
    out, squares, kept, *sent = refs
    width = left.shape[0]

    @pl.when(where[2] != tier)
    def _():
        out[...] = solved[...]

    @pl.when(where[2] == tier)
    def _():
        value = applied(halves[2], halves[3], *operands(doubled(left[...])))
        out[...] = value.T[:width]
        kept[...] = value
        own = jnp.sum(value * value, axis=0, keepdims=True)
        squares[...] = jnp.broadcast_to(own, squares.shape)
        if sent:
            tail_of(None, panel, *operands(value), width, sent[0])
            if last:
                with_squares(sent[0], width, squares)


def solve(where, tier, left, halves, solved, panel=None, last=False):
    width, rows = left.shape
    with_tail = panel is not None
    return pl.pallas_call(
        functools.partial(solve_kernel, tier, last, with_tail),
        out_shape=[shaped(width, rows), shaped(8, 2 * width), shaped(rows, 2 * width)]
        + [shaped(width + 8 * last, rows)] * with_tail,
        in_specs=[SMEM] + [VMEM] * (3 + with_tail),
        out_specs=[VMEM] * (3 + with_tail),
        cost_estimate=cost(1),
        compiler_params=limit(8),
    )(where, left, in_vmem(halves), solved, *([in_vmem(panel)] if with_tail else []))


def tails_kernel(tier, where, value, squares, panels, *refs):
    sent, (held, arrived) = refs[:-2], refs[-2:]
    width = squares.shape[1] // 2

    @pl.when(where[2] == tier)
    def _():
        copies = [
            pieces(panels.at[0, 2 + step], held.at[step], arrived.at[step])
            for step in range(held.shape[0])
        ]
        both, high = operands(value[...])
        for step, out in enumerate(sent):
            tail_of(copies[step], held.at[step], both, high, width, out)
        with_squares(sent[-1], width, squares)


def more_tails(where, tier, value, squares, panels, count):
    rows = value.shape[0]
    width = squares.shape[1] // 2
    shapes = [(width + 8 * (step == count - 1), rows) for step in range(count)]
    return pl.pallas_call(
        functools.partial(tails_kernel, tier),
        out_shape=[shaped(*shape) for shape in shapes],
        in_specs=[SMEM, VMEM, VMEM, HBM],
        out_specs=[VMEM] * count,
        scratch_shapes=[
            pltpu.VMEM((count, rows, rows), jnp.float32),
            pltpu.SemaphoreType.DMA((count, rows // PIECE)),
        ],
        cost_estimate=cost(1),
        compiler_params=limit(8 + 4 * count),
    )(where, value, squares, in_hbm(panels))


def last_kernel(leaves, count, where, own_rhs, halves, squares, got, first, second, kept, widths):

    @pl.when(where[1] != leaves - 1)
    def _():
        widths[...] = jnp.zeros_like(widths)

    @pl.when(where[1] == leaves - 1)
    def _():
        left = left_of(own_rhs, (first, second))
        value = applied(halves[2], halves[3], *operands(doubled(left)))
        kept[...] = value
        total = (squares[...] + got[...]) + jnp.sum(value * value, axis=0, keepdims=True)
        widths[...] = jnp.sqrt(total / count + 1e-06)


def last(leaves, count, where, own_rhs, halves, squares, got, parts):
    width, rows = own_rhs.shape
    return pl.pallas_call(
        functools.partial(last_kernel, leaves, count),
        out_shape=(shaped(rows, 2 * width), shaped(*squares.shape)),
        in_specs=[SMEM] + [VMEM] * 6,
        out_specs=(VMEM, VMEM),
        cost_estimate=cost(1),
        compiler_params=limit(8),
    )(where, own_rhs, in_vmem(halves), squares, got, *parts)


def settle_kernel(tiers, where, solved, value, out):
    width = out.shape[0]

    @pl.when(where[2] == tiers)
    def _():
        out[...] = value[...].T[:width]

    @pl.when(where[2] != tiers)
    def _():
        out[...] = solved[...]


def settled(tiers, where, solved, value):
    return pl.pallas_call(
        functools.partial(settle_kernel, tiers),
        out_shape=shaped(*solved.shape),
        in_specs=[SMEM, VMEM, VMEM],
        out_specs=VMEM,
        cost_estimate=cost(1),
        compiler_params=limit(6),
    )(where, solved, value)


def local(rhs_rows, order, leaf_inverse, leaf_panels, panel_mask, sep_rhs, sep_inverse, sep_panels):
    n_leaf = lax.axis_size("leaf")
    n_grid = lax.axis_size("grid")
    tiers = leaf_panels.shape[1]
    block_rows, columns = rhs_rows.shape
    block_count = n_leaf * n_grid
    sep_rows = sep_rhs.shape[1]
    width = columns // n_grid
    leaf = lax.axis_index("leaf").astype(jnp.int32)
    grid = lax.axis_index("grid").astype(jnp.int32)
    level = jnp.ones((), jnp.int32)
    for bit in range(1, tiers):
        level = level + ((leaf + 1) & (2**bit - 1) == 0).astype(jnp.int32)
    where = jnp.stack([grid, leaf, level])
    scale = jnp.repeat(panel_mask[0].astype(jnp.float32), 128, axis=1)

    picked = pick(rhs_rows, order)
    picked, where = lax.optimization_barrier((picked, where))
    moved = lax.all_to_all(
        picked.reshape(block_count, block_rows // block_count, columns),
        ("leaf", "grid"),
        split_axis=0,
        concat_axis=0,
        tiled=True,
    )
    permuted = moved.reshape(block_rows, columns)

    _, inverse, own_panels = lax.optimization_barrier((picked, sep_inverse, sep_panels))
    halves = prepared(inverse, own_panels)
    permuted, halves = lax.optimization_barrier((permuted, halves))

    given, kept = two_products(where, leaf_inverse, permuted, True)
    in_chip = lax.ppermute(given, "grid", [(0, 1), (1, 0), (2, 3)])
    onward = kept + in_chip
    onward, permuted, halves = lax.optimization_barrier((onward, permuted, halves))
    between = lax.ppermute(onward, "grid", [(0, 2), (1, 3)])
    *low_block, lowest = two_products(where, leaf_inverse, permuted, False)
    from_pair = [lax.ppermute(part, "grid", [(0, 1)]) for part in low_block]
    halves, panels = loaded(halves, leaf_panels)

    leaf_y, turned, squares, given, kept = first_update(
        where, (kept, in_chip, between, lowest, *low_block, *from_pair), scale, panels
    )
    swap = [(0, 1), (1, 0), (2, 3), (3, 2)]
    over = [(0, 2), (1, 3), (2, 0), (3, 1)]
    got = lax.ppermute(given, "grid", swap)
    given, other = second_update(where, turned, scale, panels)
    own, away = chip_sum(where, kept, got)
    away, given, turned = lax.optimization_barrier((away, given, turned))
    got = lax.ppermute(away, "grid", over)
    second, away = chip_sum(where, other, lax.ppermute(given, "grid", swap))
    given, kept = later_updates(where, squares, turned, scale, panels)
    got, away, given = lax.optimization_barrier((got, away, given))
    mine = own + got
    following = second + lax.ppermute(away, "grid", over)
    own, away = chip_sum(where, kept, lax.ppermute(given, "grid", swap))
    pairs = [(base + 1, base) for base in range(0, n_leaf, 2)]
    own, own_panels = lax.optimization_barrier((own, sep_panels))
    next_panel = loaded_panel(own_panels)
    got, own, next_panel = lax.optimization_barrier(
        (lax.ppermute(mine, "leaf", pairs), own, next_panel)
    )
    parts = [mine, got]
    edges = [(step * width, (step + 1) * width) for step in range(tiers - 2)]
    edges[-1] = (edges[-1][0], own.shape[0])
    rest = [
        own[start:stop] + lax.ppermute(away[start:stop], "grid", over) for start, stop in edges
    ]

    own_rhs = sep_rhs[0].T
    solved = jnp.zeros_like(own_rhs)
    waiting = []
    for tier in range(1, tiers):
        size = 2**tier
        direct_left, direct_right, early, onward, aside = [], [], [], [], []
        for base in range(0, n_leaf, size):
            host, end = (base + size // 2 - 1, base + size - 1)
            parent = base // (2 * size) * 2 * size + size - 1
            onward.append((host, end))
            if end == parent:
                direct_left.append((host, parent))
            else:
                direct_right.append((host, parent))
                early.append((end, parent))
                aside.append((host, end))
        left, term = direct(where, tier, own_rhs, halves, parts)
        count = len(rest)
        solved, own, *more = solve(
            where, tier, left, halves, solved, next_panel if count else None, count == 1
        )
        if waiting:
            _, following, *waiting = lax.optimization_barrier((left, following, *waiting))
            rest = [
                other + lax.ppermute(other + tail, "leaf", before)
                for other, tail in zip(rest, waiting)
            ]
        if count:
            value, tail = more
            if tier > 1:
                term, tail = lax.optimization_barrier((term, tail))
            term = following + term
            from_left = lax.ppermute(term, "leaf", direct_left)
            if tier == 1:
                turn, tail = lax.optimization_barrier((lax.ppermute(term, "leaf", aside), tail))
                parts = [following, lax.ppermute(following + turn, "leaf", early), from_left]
            else:
                next_early = lax.ppermute(following, "leaf", early)
                next_early, rest[0] = lax.optimization_barrier((next_early, rest[0]))
                from_right = lax.ppermute(term, "leaf", direct_right)
                parts = [following, next_early, from_left, from_right]
            following = rest[0] + lax.ppermute(rest[0] + tail, "leaf", onward)
            rest = rest[1:]
            waiting = []
            if count > 1:
                value, _ = lax.optimization_barrier((value, from_left))
                waiting = more_tails(where, tier, value, own, sep_panels, count - 1)
                parts[1], *waiting = lax.optimization_barrier((parts[1], *waiting))
            before = onward
        else:
            squares = following[width:, : 2 * width]
            following = following[:width]
            parts = [following, lax.ppermute(following + term, "leaf", direct_left)]
            got = lax.ppermute(squares + own, "leaf", direct_left)
    value, widths = last(
        n_leaf,
        n_leaf * (block_rows * n_grid + sep_rows),
        where,
        own_rhs,
        halves,
        squares,
        got,
        parts,
    )
    solved = settled(tiers, where, solved, value)
    step = n_leaf
    while step > 1:
        half_step = step // 2
        steps = [(end, end - half_step) for end in range(step - 1, n_leaf, step)]
        widths = widths + lax.ppermute(widths, "leaf", steps)
        step = half_step
    return (leaf_y, solved.T[None], widths[0, :width])


def solution(mesh):
    placed = (
        P(("leaf", "grid"), None),
        P(("leaf", "grid")),
        P("leaf", "grid"),
        P("leaf", None, None, "grid"),
        P("leaf", None, "grid"),
        P("leaf", None, "grid"),
        P("leaf", None, None),
        P("leaf", None, None, None),
    )
    return jax.shard_map(
        local,
        mesh=mesh,
        in_specs=placed,
        out_specs=(P(("leaf", "grid"), None), P("leaf", None, "grid"), P("grid")),
        check_vma=False,
    )
```

```python
import functools

import jax
import jax.numpy as jnp
from jax import lax
from jax.experimental import pallas as pl
from jax.experimental.pallas import tpu as pltpu
from jax.sharding import PartitionSpec as P

HIGH = lax.Precision.HIGH
SMEM = pl.BlockSpec(memory_space=pltpu.SMEM)
VMEM = pl.BlockSpec(memory_space=pltpu.VMEM)
HBM = pl.BlockSpec(memory_space=pl.ANY)
PIECE = 128
MIB = 2**20


def shaped(*shape, dtype=jnp.float32):
    return jax.ShapeDtypeStruct(shape, dtype)


def cost(products):
    return pl.CostEstimate(flops=24 * products, bytes_accessed=4 * 2**20, transcendentals=0)


def limit(mebibytes):
    return pltpu.CompilerParams(vmem_limit_bytes=mebibytes * MIB)


def split(value):
    high = value.astype(jnp.bfloat16)
    return high, (value - high.astype(jnp.float32)).astype(jnp.bfloat16)


def split_wide(value):
    high = value.astype(jnp.bfloat16)
    return high, value - high.astype(jnp.float32)


def in_hbm(value):
    return pltpu.with_memory_space_constraint(value, pltpu.HBM)


def in_vmem(value):
    return pltpu.with_memory_space_constraint(value, pltpu.VMEM)


def pieces(source, held, arrived):
    copies = []
    for step in range(held.shape[0] // PIECE):
        at = pl.ds(step * PIECE, PIECE)
        copies.append(pltpu.make_async_copy(source.at[at], held.at[at], arrived.at[step]))
        copies[step].start()
    return copies


def wait(copies, rows):
    for copy in copies[rows.start // PIECE : rows.stop // PIECE]:
        copy.wait()


def whole(*shape):
    return pl.BlockSpec(shape, lambda *step: (0,) * len(shape))


def pick_kernel(order, rows, out):
    size = rows.shape[0]
    place = lax.broadcasted_iota(jnp.int32, (size, size), 0)
    chosen = jnp.where(place == order[...], 1.0, 0.0).T.astype(jnp.bfloat16)
    high, rest = split_wide(rows[...])
    middle, low = split(rest)
    value = jnp.dot(chosen, high, preferred_element_type=jnp.float32)
    value = value + jnp.dot(chosen, middle, preferred_element_type=jnp.float32)
    out[...] = value + jnp.dot(chosen, low, preferred_element_type=jnp.float32)


def pick(rows, order):
    size, columns = rows.shape
    return pl.pallas_call(
        pick_kernel,
        out_shape=shaped(size, columns),
        grid=(1,),
        in_specs=[whole(1, size), whole(size, columns)],
        out_specs=whole(size, columns),
        cost_estimate=cost(size * size * columns),
        compiler_params=limit(12),
    )(in_hbm(order.reshape(1, size)), in_hbm(rows))


def product_kernel(last_two, place, matrix, rows, *outs):
    size = rows.shape[0]
    for step in range(2):
        block = 2 + ((place[0] & 1) ^ (1 - step)) if last_two else 1 - step
        at = pl.ds(pl.multiple_of(block * size, size), size)
        value = jnp.dot(
            matrix[at], rows[...], precision=HIGH, preferred_element_type=jnp.float32
        )
        if last_two:
            outs[step][...] = value
        elif step == 0:
            outs[0][...] = value[: size // 2]
            outs[1][...] = value[size // 2 :]
        else:
            outs[2][...] = value


def two_products(place, matrix, rows, last_two):
    size, columns = rows.shape
    shapes = [size, size] if last_two else [size // 2, size // 2, size]
    return pl.pallas_call(
        functools.partial(product_kernel, last_two),
        out_shape=[shaped(count, columns) for count in shapes],
        in_specs=[SMEM, VMEM, VMEM],
        out_specs=[VMEM] * len(shapes),
        cost_estimate=cost(2 * size * size * columns),
        compiler_params=limit(8),
    )(place, in_vmem(matrix), rows)


def update_of(turned, scale, panel):
    return lax.dot_general(
        turned * scale,
        panel,
        (((1,), (1,)), ((), ())),
        precision=HIGH,
        preferred_element_type=jnp.float32,
    )


def hand_out(value, core, rows, lanes, width, given, kept):
    for mine in range(2):

        @pl.when(core == mine)
        def _(mine=mine):
            for half in range(2):
                at = (2 * half + mine) * width
                other = (2 * half + 1 - mine) * width
                kept[half, rows, lanes] = value[at : at + width]
                given[half, rows, lanes] = value[other : other + width]


def first_update_kernel(
    width, where, kept_in, in_chip, between, lowest, top, bottom, pair_top, pair_bottom, scale, panels,
    leaf_y, turned, squares, given, kept
):
    place = where[0]

    @pl.when(place == 0)
    def _():
        leaf_y[...] = lowest[...]

    @pl.when(place == 1)
    def _():
        middle = leaf_y.shape[0] // 2
        leaf_y[:middle] = top[...] + pair_top[...]
        leaf_y[middle:] = bottom[...] + pair_bottom[...]

    @pl.when(place == 2)
    def _():
        leaf_y[...] = kept_in[...] + between[...]

    @pl.when(place == 3)
    def _():
        leaf_y[...] = (kept_in[...] + in_chip[...]) + between[...]

    turned[...] = leaf_y[...].T
    value = update_of(turned[...], scale[0:1], panels[0])
    hand_out(value, place & 1, slice(None), slice(None), width, given, kept)
    own = jnp.sum(leaf_y[...] * leaf_y[...], axis=0, keepdims=True)
    squares[...] = jnp.broadcast_to(own, squares.shape)


def first_update(where, parts, scale, panels):
    size, columns = parts[0].shape
    rows = panels.shape[1]
    width = columns // 4
    halves = shaped(2, width, rows)
    return pl.pallas_call(
        functools.partial(first_update_kernel, width),
        out_shape=(
            shaped(size, columns), shaped(columns, size), shaped(8, columns), halves, halves
        ),
        in_specs=[SMEM] + [VMEM] * (len(parts) + 2),
        out_specs=(VMEM,) * 5,
        cost_estimate=cost(size * rows * columns),
        compiler_params=limit(12),
    )(where, *parts, scale, in_vmem(panels))


def second_update_kernel(width, where, turned, scale, panels, given, kept):
    every = slice(None)
    value = update_of(turned[...], scale[1:2], panels[1])
    hand_out(value, where[0] & 1, every, every, width, given, kept)


def second_update(where, turned, scale, panels):
    columns, size = turned.shape
    rows = panels.shape[1]
    width = columns // 4
    halves = shaped(2, width, rows)
    return pl.pallas_call(
        functools.partial(second_update_kernel, width),
        out_shape=(halves, halves),
        in_specs=[SMEM] + [VMEM] * 3,
        out_specs=(VMEM, VMEM),
        cost_estimate=cost(size * rows * columns),
        compiler_params=limit(8),
    )(where, turned, scale, in_vmem(panels))


def later_update_kernel(width, where, squares, turned, scale, panels, given, kept):
    core = where[0] & 1
    tiers = panels.shape[0]
    for tier in range(2, tiers):
        value = update_of(turned[...], scale[tier : tier + 1], panels[tier])
        rows = slice((tier - 2) * width, (tier - 1) * width)
        hand_out(value, core, rows, slice(None), width, given, kept)
    at = (tiers - 2) * width
    for refs, of in ((given, 1 - core), (kept, core)):
        refs[:, at:, :] = jnp.zeros((2, 8, refs.shape[2]), jnp.float32)
        for half in range(2):
            pair = squares[:, 2 * width * half : 2 * width * (half + 1)]
            pair = jnp.where(of == 0, pair, pltpu.roll(pair, width, 1))
            refs[half, at:, 0 : 2 * width] = pair


def later_updates(where, squares, turned, scale, panels):
    columns, size = turned.shape
    tiers, rows = panels.shape[:2]
    width = columns // 4
    halves = shaped(2, (tiers - 2) * width + 8, rows)
    return pl.pallas_call(
        functools.partial(later_update_kernel, width),
        out_shape=(halves, halves),
        in_specs=[SMEM] + [VMEM] * 4,
        out_specs=(VMEM, VMEM),
        cost_estimate=cost(1),
        compiler_params=limit(12),
    )(where, squares, turned, scale, in_vmem(panels))


def chip_sum_kernel(where, kept, got, own, away):
    half = where[0] >> 1
    own[...] = kept[half] + got[half]
    away[...] = kept[1 - half] + got[1 - half]


def chip_sum(where, kept, got):
    shape = shaped(*kept.shape[1:])
    return pl.pallas_call(
        chip_sum_kernel,
        out_shape=(shape, shape),
        in_specs=[SMEM, VMEM, VMEM],
        out_specs=(VMEM, VMEM),
        cost_estimate=cost(1),
        compiler_params=limit(6),
    )(where, kept, got)


def prepare_kernel(
    inverse, panels, out, wide, direct_high, direct_low, high, low, inverse_arrived, panel_arrived, gone
):
    rows = high.shape[0]
    block = rows // 4
    copies = pieces(inverse.at[0], wide.at[0], inverse_arrived)
    pieces(panels.at[0, 0], wide.at[1], panel_arrived)
    for at in range(0, rows, block):
        part = slice(at, at + block)
        wait(copies, part)
        high[part], low[part] = split(wide[0, part])
    sent = [
        pltpu.make_async_copy(source, out.at[2 + step], gone.at[step])
        for step, source in enumerate((high, low))
    ]
    for copy in sent:
        copy.start()

    def part_sent(step):
        part = pl.ds(pl.multiple_of(step * block, block), block)
        return [
            pltpu.make_async_copy(source.at[part], out.at[which, part], gone.at[2 + which])
            for which, source in enumerate((direct_high, direct_low))
        ]

    @pl.loop(0, 4)
    def _(step):
        part = pl.ds(pl.multiple_of(step * block, block), block)
        for piece in range(block // PIECE):
            at = pl.ds(pl.multiple_of(step * block + piece * PIECE, PIECE), PIECE)
            pltpu.make_async_copy(
                panels.at[0, 0, at], wide.at[1, at], panel_arrived.at[step * (block // PIECE) + piece]
            ).wait()
        panel_high, panel_low = split(wide[1, part])
        for at in range(0, rows, block):
            lanes = slice(at, at + block)
            both = high[at:, lanes]
            value = jnp.dot(panel_high[:, at:], both, preferred_element_type=jnp.float32)
            value = value + jnp.dot(panel_low[:, at:], both, preferred_element_type=jnp.float32)
            value = value + jnp.dot(
                panel_high[:, at:], low[at:, lanes], preferred_element_type=jnp.float32
            )
            direct_high[part, lanes], direct_low[part, lanes] = split(value)

        @pl.when(step > 0)
        def _():
            for copy in part_sent(step - 1):
                copy.wait()

        for copy in part_sent(step):
            copy.start()

    for copy in sent + part_sent(3):
        copy.wait()


def prepared(sep_inverse, sep_panels):
    rows = sep_inverse.shape[1]
    return pl.pallas_call(
        prepare_kernel,
        out_shape=pltpu.HBM((4, rows, rows), jnp.bfloat16),
        in_specs=[HBM] * 2,
        out_specs=HBM,
        scratch_shapes=[pltpu.VMEM((2, rows, rows), jnp.float32)]
        + [pltpu.VMEM((rows, rows), jnp.bfloat16)] * 4
        + [
            pltpu.SemaphoreType.DMA((rows // PIECE,)),
            pltpu.SemaphoreType.DMA((rows // PIECE,)),
            pltpu.SemaphoreType.DMA((4,)),
        ],
        cost_estimate=cost(rows**3),
        compiler_params=limit(24),
    )(in_hbm(sep_inverse), in_hbm(sep_panels))


def load_kernel(halves, panels, halves_out, panels_out, arrived):
    copies = [(panels.at[0, step], panels_out.at[step]) for step in range(panels_out.shape[0])]
    copies += [(halves.at[step], halves_out.at[step]) for step in range(4)]
    copies = [
        pltpu.make_async_copy(source, target, arrived.at[step])
        for step, (source, target) in enumerate(copies)
    ]
    for copy in copies:
        copy.start()
    for copy in copies:
        copy.wait()


def loaded(halves, leaf_panels):
    return pl.pallas_call(
        load_kernel,
        out_shape=(
            pltpu.VMEM(halves.shape, jnp.bfloat16),
            pltpu.VMEM(leaf_panels.shape[1:], jnp.float32),
        ),
        in_specs=[HBM] * 2,
        out_specs=(VMEM,) * 2,
        scratch_shapes=[pltpu.SemaphoreType.DMA((4 + leaf_panels.shape[1],))],
        cost_estimate=cost(1),
        compiler_params=limit(4),
    )(in_hbm(halves), in_hbm(leaf_panels))


def load_panel_kernel(panels, out, arrived):
    copies = pieces(panels.at[0, 1], out, arrived)
    wait(copies, slice(0, out.shape[0]))


def loaded_panel(panels):
    rows = panels.shape[2]
    return pl.pallas_call(
        load_panel_kernel,
        out_shape=pltpu.VMEM(panels.shape[2:], jnp.float32),
        in_specs=[HBM],
        out_specs=VMEM,
        scratch_shapes=[pltpu.SemaphoreType.DMA((rows // PIECE,))],
        cost_estimate=cost(1),
        compiler_params=limit(4),
    )(in_hbm(panels))


def operands(value):
    width = value.shape[1] // 2
    lane = lax.broadcasted_iota(jnp.int32, value.shape, 1)
    high = value.astype(jnp.bfloat16)
    as_wide = high.astype(jnp.float32)
    return jnp.where(lane < width, as_wide, value - as_wide).astype(jnp.bfloat16), high


def applied(matrix_high, matrix_low, both, high):
    first = jnp.dot(matrix_high, both, preferred_element_type=jnp.float32)
    second = jnp.dot(matrix_low, high, preferred_element_type=jnp.float32)
    return (first + pltpu.roll(first, first.shape[1] // 2, 1)) + second


def doubled(value):
    return jnp.concatenate([value, value], axis=0).T


def left_of(own_rhs, parts):
    total = parts[0][...]
    for part in parts[1:]:
        total = total + part[...]
    return own_rhs[...] - total


def direct_kernel(tier, count, where, own_rhs, halves, *refs):
    parts, (left, term) = refs[:count], refs[count:]

    @pl.when(where[2] == tier)
    def _():
        left[...] = left_of(own_rhs, parts)
        value = applied(halves[0], halves[1], *operands(doubled(left[...])))
        term[...] = value.T[: term.shape[0]]


def direct(where, tier, own_rhs, halves, parts):
    width, rows = own_rhs.shape
    return pl.pallas_call(
        functools.partial(direct_kernel, tier, len(parts)),
        out_shape=(shaped(width, rows), shaped(width, rows)),
        in_specs=[SMEM] + [VMEM] * (2 + len(parts)),
        out_specs=(VMEM, VMEM),
        cost_estimate=cost(rows**2 * 64),
        compiler_params=limit(8),
    )(where, own_rhs, in_vmem(halves), *parts)


def tail_of(copies, held, both, high, width, out):
    rows = held.shape[0]
    block = rows // 4
    for at in range(0, rows, block):
        part = slice(at, at + block)
        if copies:
            wait(copies, part)
        out[:width, part] = applied(*split(held[part]), both, high).T[:width]


def with_squares(out, width, squares):
    out[width:, :] = jnp.zeros((8, out.shape[1]), jnp.float32)
    out[width:, : squares.shape[1]] = squares[...]


def solve_kernel(tier, last, with_tail, where, left, halves, solved, *refs):
    panel, refs = refs[0] if with_tail else None, refs[with_tail:]
    out, squares, kept, *sent = refs
    width = left.shape[0]

    @pl.when(where[2] != tier)
    def _():
        out[...] = solved[...]

    @pl.when(where[2] == tier)
    def _():
        value = applied(halves[2], halves[3], *operands(doubled(left[...])))
        out[...] = value.T[:width]
        kept[...] = value
        own = jnp.sum(value * value, axis=0, keepdims=True)
        squares[...] = jnp.broadcast_to(own, squares.shape)
        if sent:
            tail_of(None, panel, *operands(value), width, sent[0])
            if last:
                with_squares(sent[0], width, squares)


def solve(where, tier, left, halves, solved, panel=None, last=False):
    width, rows = left.shape
    with_tail = panel is not None
    return pl.pallas_call(
        functools.partial(solve_kernel, tier, last, with_tail),
        out_shape=[shaped(width, rows), shaped(8, 2 * width), shaped(rows, 2 * width)]
        + [shaped(width + 8 * last, rows)] * with_tail,
        in_specs=[SMEM] + [VMEM] * (3 + with_tail),
        out_specs=[VMEM] * (3 + with_tail),
        cost_estimate=cost(1),
        compiler_params=limit(8),
    )(where, left, in_vmem(halves), solved, *([in_vmem(panel)] if with_tail else []))


def tails_kernel(tier, where, value, squares, panels, *refs):
    sent, (held, arrived) = refs[:-2], refs[-2:]
    width = squares.shape[1] // 2

    @pl.when(where[2] == tier)
    def _():
        copies = [
            pieces(panels.at[0, 2 + step], held.at[step], arrived.at[step])
            for step in range(held.shape[0])
        ]
        both, high = operands(value[...])
        for step, out in enumerate(sent):
            tail_of(copies[step], held.at[step], both, high, width, out)
        with_squares(sent[-1], width, squares)


def more_tails(where, tier, value, squares, panels, count):
    rows = value.shape[0]
    width = squares.shape[1] // 2
    shapes = [(width + 8 * (step == count - 1), rows) for step in range(count)]
    return pl.pallas_call(
        functools.partial(tails_kernel, tier),
        out_shape=[shaped(*shape) for shape in shapes],
        in_specs=[SMEM, VMEM, VMEM, HBM],
        out_specs=[VMEM] * count,
        scratch_shapes=[
            pltpu.VMEM((count, rows, rows), jnp.float32),
            pltpu.SemaphoreType.DMA((count, rows // PIECE)),
        ],
        cost_estimate=cost(1),
        compiler_params=limit(8 + 4 * count),
    )(where, value, squares, in_hbm(panels))


def last_kernel(leaves, count, where, own_rhs, halves, squares, got, first, second, kept, widths):

    @pl.when(where[1] != leaves - 1)
    def _():
        widths[...] = jnp.zeros_like(widths)

    @pl.when(where[1] == leaves - 1)
    def _():
        left = left_of(own_rhs, (first, second))
        value = applied(halves[2], halves[3], *operands(doubled(left)))
        kept[...] = value
        total = (squares[...] + got[...]) + jnp.sum(value * value, axis=0, keepdims=True)
        widths[...] = jnp.sqrt(total / count + 1e-06)


def last(leaves, count, where, own_rhs, halves, squares, got, parts):
    width, rows = own_rhs.shape
    return pl.pallas_call(
        functools.partial(last_kernel, leaves, count),
        out_shape=(shaped(rows, 2 * width), shaped(*squares.shape)),
        in_specs=[SMEM] + [VMEM] * 6,
        out_specs=(VMEM, VMEM),
        cost_estimate=cost(1),
        compiler_params=limit(8),
    )(where, own_rhs, in_vmem(halves), squares, got, *parts)


def settle_kernel(tiers, where, solved, value, out):
    width = out.shape[0]

    @pl.when(where[2] == tiers)
    def _():
        out[...] = value[...].T[:width]

    @pl.when(where[2] != tiers)
    def _():
        out[...] = solved[...]


def settled(tiers, where, solved, value):
    return pl.pallas_call(
        functools.partial(settle_kernel, tiers),
        out_shape=shaped(*solved.shape),
        in_specs=[SMEM, VMEM, VMEM],
        out_specs=VMEM,
        cost_estimate=cost(1),
        compiler_params=limit(6),
    )(where, solved, value)


def local(rhs_rows, order, leaf_inverse, leaf_panels, panel_mask, sep_rhs, sep_inverse, sep_panels):
    n_leaf = lax.axis_size("leaf")
    n_grid = lax.axis_size("grid")
    tiers = leaf_panels.shape[1]
    block_rows, columns = rhs_rows.shape
    block_count = n_leaf * n_grid
    sep_rows = sep_rhs.shape[1]
    width = columns // n_grid
    leaf = lax.axis_index("leaf").astype(jnp.int32)
    grid = lax.axis_index("grid").astype(jnp.int32)
    level = jnp.ones((), jnp.int32)
    for bit in range(1, tiers):
        level = level + ((leaf + 1) & (2**bit - 1) == 0).astype(jnp.int32)
    where = jnp.stack([grid, leaf, level])
    scale = jnp.repeat(panel_mask[0].astype(jnp.float32), 128, axis=1)

    picked = pick(rhs_rows, order)
    picked, where = lax.optimization_barrier((picked, where))
    moved = lax.all_to_all(
        picked.reshape(block_count, block_rows // block_count, columns),
        ("leaf", "grid"),
        split_axis=0,
        concat_axis=0,
        tiled=True,
    )
    permuted = moved.reshape(block_rows, columns)

    _, inverse, own_panels = lax.optimization_barrier((picked, sep_inverse, sep_panels))
    halves = prepared(inverse, own_panels)
    permuted, halves = lax.optimization_barrier((permuted, halves))

    given, kept = two_products(where, leaf_inverse, permuted, True)
    in_chip = lax.ppermute(given, "grid", [(0, 1), (1, 0), (2, 3)])
    onward = kept + in_chip
    onward, permuted, halves = lax.optimization_barrier((onward, permuted, halves))
    between = lax.ppermute(onward, "grid", [(0, 2), (1, 3)])
    *low_block, lowest = two_products(where, leaf_inverse, permuted, False)
    from_pair = [lax.ppermute(part, "grid", [(0, 1)]) for part in low_block]
    halves, panels = loaded(halves, leaf_panels)

    leaf_y, turned, squares, given, kept = first_update(
        where, (kept, in_chip, between, lowest, *low_block, *from_pair), scale, panels
    )
    swap = [(0, 1), (1, 0), (2, 3), (3, 2)]
    over = [(0, 2), (1, 3), (2, 0), (3, 1)]
    got = lax.ppermute(given, "grid", swap)
    given, other = second_update(where, turned, scale, panels)
    own, away = chip_sum(where, kept, got)
    away, given, turned = lax.optimization_barrier((away, given, turned))
    got = lax.ppermute(away, "grid", over)
    second, away = chip_sum(where, other, lax.ppermute(given, "grid", swap))
    given, kept = later_updates(where, squares, turned, scale, panels)
    got, away, given = lax.optimization_barrier((got, away, given))
    mine = own + got
    following = second + lax.ppermute(away, "grid", over)
    own, away = chip_sum(where, kept, lax.ppermute(given, "grid", swap))
    pairs = [(base + 1, base) for base in range(0, n_leaf, 2)]
    own, own_panels = lax.optimization_barrier((own, sep_panels))
    next_panel = loaded_panel(own_panels)
    got, own, next_panel = lax.optimization_barrier(
        (lax.ppermute(mine, "leaf", pairs), own, next_panel)
    )
    parts = [mine, got]
    edges = [(step * width, (step + 1) * width) for step in range(tiers - 2)]
    edges[-1] = (edges[-1][0], own.shape[0])
    rest = [
        own[start:stop] + lax.ppermute(away[start:stop], "grid", over) for start, stop in edges
    ]

    own_rhs = sep_rhs[0].T
    solved = jnp.zeros_like(own_rhs)
    waiting = []
    for tier in range(1, tiers):
        size = 2**tier
        direct_left, direct_right, early, onward, aside = [], [], [], [], []
        for base in range(0, n_leaf, size):
            host, end = (base + size // 2 - 1, base + size - 1)
            parent = base // (2 * size) * 2 * size + size - 1
            onward.append((host, end))
            if end == parent:
                direct_left.append((host, parent))
            else:
                direct_right.append((host, parent))
                early.append((end, parent))
                aside.append((host, end))
        left, term = direct(where, tier, own_rhs, halves, parts)
        count = len(rest)
        solved, own, *more = solve(
            where, tier, left, halves, solved, next_panel if count else None, count == 1
        )
        if waiting:
            _, following, *waiting = lax.optimization_barrier((left, following, *waiting))
            rest = [
                other + lax.ppermute(other + tail, "leaf", before)
                for other, tail in zip(rest, waiting)
            ]
        if count:
            value, tail = more
            term = following + term
            from_left = lax.ppermute(term, "leaf", direct_left)
            if tier == 1:
                turn, tail = lax.optimization_barrier((lax.ppermute(term, "leaf", aside), tail))
                parts = [following, lax.ppermute(following + turn, "leaf", early), from_left]
            else:
                next_early = lax.ppermute(following, "leaf", early)
                from_right = lax.ppermute(term, "leaf", direct_right)
                parts = [following, next_early, from_left, from_right]
            following = rest[0] + lax.ppermute(rest[0] + tail, "leaf", onward)
            rest = rest[1:]
            waiting = []
            if count > 1:
                value, _ = lax.optimization_barrier((value, from_left))
                waiting = more_tails(where, tier, value, own, sep_panels, count - 1)
                parts[1], *waiting = lax.optimization_barrier((parts[1], *waiting))
            before = onward
        else:
            squares = following[width:, : 2 * width]
            following = following[:width]
            parts = [following, lax.ppermute(following + term, "leaf", direct_left)]
            got = lax.ppermute(squares + own, "leaf", direct_left)
    value, widths = last(
        n_leaf,
        n_leaf * (block_rows * n_grid + sep_rows),
        where,
        own_rhs,
        halves,
        squares,
        got,
        parts,
    )
    solved = settled(tiers, where, solved, value)
    step = n_leaf
    while step > 1:
        half_step = step // 2
        steps = [(end, end - half_step) for end in range(step - 1, n_leaf, step)]
        widths = widths + lax.ppermute(widths, "leaf", steps)
        step = half_step
    return (leaf_y, solved.T[None], widths[0, :width])


def solution(mesh):
    placed = (
        P(("leaf", "grid"), None),
        P(("leaf", "grid")),
        P("leaf", "grid"),
        P("leaf", None, None, "grid"),
        P("leaf", None, "grid"),
        P("leaf", None, "grid"),
        P("leaf", None, None),
        P("leaf", None, None, None),
    )
    return jax.shard_map(
        local,
        mesh=mesh,
        in_specs=placed,
        out_specs=(P(("leaf", "grid"), None), P("leaf", None, "grid"), P("grid")),
        check_vma=False,
    )
```

```python
import functools

import jax
import jax.numpy as jnp
from jax import lax
from jax.experimental import pallas as pl
from jax.experimental.pallas import tpu as pltpu
from jax.sharding import PartitionSpec as P

HIGH = lax.Precision.HIGH
SMEM = pl.BlockSpec(memory_space=pltpu.SMEM)
VMEM = pl.BlockSpec(memory_space=pltpu.VMEM)
HBM = pl.BlockSpec(memory_space=pl.ANY)
PIECE = 128
MIB = 2**20


def shaped(*shape, dtype=jnp.float32):
    return jax.ShapeDtypeStruct(shape, dtype)


def cost(products):
    return pl.CostEstimate(flops=24 * products, bytes_accessed=4 * 2**20, transcendentals=0)


def limit(mebibytes):
    return pltpu.CompilerParams(vmem_limit_bytes=mebibytes * MIB)


def split(value):
    high = value.astype(jnp.bfloat16)
    return high, (value - high.astype(jnp.float32)).astype(jnp.bfloat16)


def split_wide(value):
    high = value.astype(jnp.bfloat16)
    return high, value - high.astype(jnp.float32)


def in_hbm(value):
    return pltpu.with_memory_space_constraint(value, pltpu.HBM)


def in_vmem(value):
    return pltpu.with_memory_space_constraint(value, pltpu.VMEM)


def pieces(source, held, arrived):
    copies = []
    for step in range(held.shape[0] // PIECE):
        at = pl.ds(step * PIECE, PIECE)
        copies.append(pltpu.make_async_copy(source.at[at], held.at[at], arrived.at[step]))
        copies[step].start()
    return copies


def wait(copies, rows):
    for copy in copies[rows.start // PIECE : rows.stop // PIECE]:
        copy.wait()


def whole(*shape):
    return pl.BlockSpec(shape, lambda *step: (0,) * len(shape))


def pick_kernel(order, rows, out):
    size = rows.shape[0]
    place = lax.broadcasted_iota(jnp.int32, (size, size), 0)
    chosen = jnp.where(place == order[...], 1.0, 0.0).T.astype(jnp.bfloat16)
    high, rest = split_wide(rows[...])
    middle, low = split(rest)
    value = jnp.dot(chosen, high, preferred_element_type=jnp.float32)
    value = value + jnp.dot(chosen, middle, preferred_element_type=jnp.float32)
    out[...] = value + jnp.dot(chosen, low, preferred_element_type=jnp.float32)


def pick(rows, order):
    size, columns = rows.shape
    return pl.pallas_call(
        pick_kernel,
        out_shape=shaped(size, columns),
        grid=(1,),
        in_specs=[whole(1, size), whole(size, columns)],
        out_specs=whole(size, columns),
        cost_estimate=cost(size * size * columns),
        compiler_params=limit(12),
    )(in_hbm(order.reshape(1, size)), in_hbm(rows))


def product_kernel(last_two, place, matrix, rows, *outs):
    size = rows.shape[0]
    for step in range(2):
        block = 2 + ((place[0] & 1) ^ (1 - step)) if last_two else 1 - step
        at = pl.ds(pl.multiple_of(block * size, size), size)
        value = jnp.dot(
            matrix[at], rows[...], precision=HIGH, preferred_element_type=jnp.float32
        )
        if last_two:
            outs[step][...] = value
        elif step == 0:
            outs[0][...] = value[: size // 2]
            outs[1][...] = value[size // 2 :]
        else:
            outs[2][...] = value


def two_products(place, matrix, rows, last_two):
    size, columns = rows.shape
    shapes = [size, size] if last_two else [size // 2, size // 2, size]
    return pl.pallas_call(
        functools.partial(product_kernel, last_two),
        out_shape=[shaped(count, columns) for count in shapes],
        in_specs=[SMEM, VMEM, VMEM],
        out_specs=[VMEM] * len(shapes),
        cost_estimate=cost(2 * size * size * columns),
        compiler_params=limit(8),
    )(place, in_vmem(matrix), rows)


def update_of(turned, scale, panel):
    return lax.dot_general(
        turned * scale,
        panel,
        (((1,), (1,)), ((), ())),
        precision=HIGH,
        preferred_element_type=jnp.float32,
    )


def hand_out(value, core, rows, lanes, width, given, kept):
    for mine in range(2):

        @pl.when(core == mine)
        def _(mine=mine):
            for half in range(2):
                at = (2 * half + mine) * width
                other = (2 * half + 1 - mine) * width
                kept[half, rows, lanes] = value[at : at + width]
                given[half, rows, lanes] = value[other : other + width]


def first_update_kernel(
    width, where, kept_in, in_chip, between, lowest, top, bottom, pair_top, pair_bottom, scale, panels,
    leaf_y, turned, squares, given, kept
):
    place = where[0]

    @pl.when(place == 0)
    def _():
        leaf_y[...] = lowest[...]

    @pl.when(place == 1)
    def _():
        middle = leaf_y.shape[0] // 2
        leaf_y[:middle] = top[...] + pair_top[...]
        leaf_y[middle:] = bottom[...] + pair_bottom[...]

    @pl.when(place == 2)
    def _():
        leaf_y[...] = kept_in[...] + between[...]

    @pl.when(place == 3)
    def _():
        leaf_y[...] = (kept_in[...] + in_chip[...]) + between[...]

    turned[...] = leaf_y[...].T
    value = update_of(turned[...], scale[0:1], panels[0])
    hand_out(value, place & 1, slice(None), slice(None), width, given, kept)
    own = jnp.sum(leaf_y[...] * leaf_y[...], axis=0, keepdims=True)
    squares[...] = jnp.broadcast_to(own, squares.shape)


def first_update(where, parts, scale, panels):
    size, columns = parts[0].shape
    rows = panels.shape[1]
    width = columns // 4
    halves = shaped(2, width, rows)
    return pl.pallas_call(
        functools.partial(first_update_kernel, width),
        out_shape=(
            shaped(size, columns), shaped(columns, size), shaped(8, columns), halves, halves
        ),
        in_specs=[SMEM] + [VMEM] * (len(parts) + 2),
        out_specs=(VMEM,) * 5,
        cost_estimate=cost(size * rows * columns),
        compiler_params=limit(12),
    )(where, *parts, scale, in_vmem(panels))


def second_update_kernel(width, where, turned, scale, panels, given, kept):
    every = slice(None)
    value = update_of(turned[...], scale[1:2], panels[1])
    hand_out(value, where[0] & 1, every, every, width, given, kept)


def second_update(where, turned, scale, panels):
    columns, size = turned.shape
    rows = panels.shape[1]
    width = columns // 4
    halves = shaped(2, width, rows)
    return pl.pallas_call(
        functools.partial(second_update_kernel, width),
        out_shape=(halves, halves),
        in_specs=[SMEM] + [VMEM] * 3,
        out_specs=(VMEM, VMEM),
        cost_estimate=cost(size * rows * columns),
        compiler_params=limit(8),
    )(where, turned, scale, in_vmem(panels))


def later_update_kernel(width, where, squares, turned, scale, panels, given, kept):
    core = where[0] & 1
    tiers = panels.shape[0]
    for tier in range(2, tiers):
        value = update_of(turned[...], scale[tier : tier + 1], panels[tier])
        rows = slice((tier - 2) * width, (tier - 1) * width)
        hand_out(value, core, rows, slice(None), width, given, kept)
    at = (tiers - 2) * width
    for refs, of in ((given, 1 - core), (kept, core)):
        refs[:, at:, :] = jnp.zeros((2, 8, refs.shape[2]), jnp.float32)
        for half in range(2):
            pair = squares[:, 2 * width * half : 2 * width * (half + 1)]
            pair = jnp.where(of == 0, pair, pltpu.roll(pair, width, 1))
            refs[half, at:, 0 : 2 * width] = pair


def later_updates(where, squares, turned, scale, panels):
    columns, size = turned.shape
    tiers, rows = panels.shape[:2]
    width = columns // 4
    halves = shaped(2, (tiers - 2) * width + 8, rows)
    return pl.pallas_call(
        functools.partial(later_update_kernel, width),
        out_shape=(halves, halves),
        in_specs=[SMEM] + [VMEM] * 4,
        out_specs=(VMEM, VMEM),
        cost_estimate=cost(1),
        compiler_params=limit(12),
    )(where, squares, turned, scale, in_vmem(panels))


def chip_sum_kernel(where, kept, got, own, away):
    half = where[0] >> 1
    own[...] = kept[half] + got[half]
    away[...] = kept[1 - half] + got[1 - half]


def chip_sum(where, kept, got):
    shape = shaped(*kept.shape[1:])
    return pl.pallas_call(
        chip_sum_kernel,
        out_shape=(shape, shape),
        in_specs=[SMEM, VMEM, VMEM],
        out_specs=(VMEM, VMEM),
        cost_estimate=cost(1),
        compiler_params=limit(6),
    )(where, kept, got)


def prepare_kernel(
    inverse, panels, out, wide, direct_high, direct_low, high, low, inverse_arrived, panel_arrived, gone
):
    rows = high.shape[0]
    block = rows // 4
    copies = pieces(inverse.at[0], wide.at[0], inverse_arrived)
    pieces(panels.at[0, 0], wide.at[1], panel_arrived)
    for at in range(0, rows, block):
        part = slice(at, at + block)
        wait(copies, part)
        high[part], low[part] = split(wide[0, part])
    sent = [
        pltpu.make_async_copy(source, out.at[2 + step], gone.at[step])
        for step, source in enumerate((high, low))
    ]
    for copy in sent:
        copy.start()

    def part_sent(step):
        part = pl.ds(pl.multiple_of(step * block, block), block)
        return [
            pltpu.make_async_copy(source.at[part], out.at[which, part], gone.at[2 + which])
            for which, source in enumerate((direct_high, direct_low))
        ]

    @pl.loop(0, 4)
    def _(step):
        part = pl.ds(pl.multiple_of(step * block, block), block)
        for piece in range(block // PIECE):
            at = pl.ds(pl.multiple_of(step * block + piece * PIECE, PIECE), PIECE)
            pltpu.make_async_copy(
                panels.at[0, 0, at], wide.at[1, at], panel_arrived.at[step * (block // PIECE) + piece]
            ).wait()
        panel_high, panel_low = split(wide[1, part])
        for at in range(0, rows, block):
            lanes = slice(at, at + block)
            both = high[at:, lanes]
            value = jnp.dot(panel_high[:, at:], both, preferred_element_type=jnp.float32)
            value = value + jnp.dot(panel_low[:, at:], both, preferred_element_type=jnp.float32)
            value = value + jnp.dot(
                panel_high[:, at:], low[at:, lanes], preferred_element_type=jnp.float32
            )
            direct_high[part, lanes], direct_low[part, lanes] = split(value)

        @pl.when(step > 0)
        def _():
            for copy in part_sent(step - 1):
                copy.wait()

        for copy in part_sent(step):
            copy.start()

    for copy in sent + part_sent(3):
        copy.wait()


def prepared(sep_inverse, sep_panels):
    rows = sep_inverse.shape[1]
    return pl.pallas_call(
        prepare_kernel,
        out_shape=pltpu.HBM((4, rows, rows), jnp.bfloat16),
        in_specs=[HBM] * 2,
        out_specs=HBM,
        scratch_shapes=[pltpu.VMEM((2, rows, rows), jnp.float32)]
        + [pltpu.VMEM((rows, rows), jnp.bfloat16)] * 4
        + [
            pltpu.SemaphoreType.DMA((rows // PIECE,)),
            pltpu.SemaphoreType.DMA((rows // PIECE,)),
            pltpu.SemaphoreType.DMA((4,)),
        ],
        cost_estimate=cost(rows**3),
        compiler_params=limit(24),
    )(in_hbm(sep_inverse), in_hbm(sep_panels))


def load_kernel(halves, panels, halves_out, panels_out, arrived):
    copies = [(panels.at[0, step], panels_out.at[step]) for step in range(panels_out.shape[0])]
    copies += [(halves.at[step], halves_out.at[step]) for step in range(4)]
    copies = [
        pltpu.make_async_copy(source, target, arrived.at[step])
        for step, (source, target) in enumerate(copies)
    ]
    for copy in copies:
        copy.start()
    for copy in copies:
        copy.wait()


def loaded(halves, leaf_panels):
    return pl.pallas_call(
        load_kernel,
        out_shape=(
            pltpu.VMEM(halves.shape, jnp.bfloat16),
            pltpu.VMEM(leaf_panels.shape[1:], jnp.float32),
        ),
        in_specs=[HBM] * 2,
        out_specs=(VMEM,) * 2,
        scratch_shapes=[pltpu.SemaphoreType.DMA((4 + leaf_panels.shape[1],))],
        cost_estimate=cost(1),
        compiler_params=limit(4),
    )(in_hbm(halves), in_hbm(leaf_panels))


def load_panel_kernel(panels, out, arrived):
    copies = pieces(panels.at[0, 1], out, arrived)
    wait(copies, slice(0, out.shape[0]))


def loaded_panel(panels):
    rows = panels.shape[2]
    return pl.pallas_call(
        load_panel_kernel,
        out_shape=pltpu.VMEM(panels.shape[2:], jnp.float32),
        in_specs=[HBM],
        out_specs=VMEM,
        scratch_shapes=[pltpu.SemaphoreType.DMA((rows // PIECE,))],
        cost_estimate=cost(1),
        compiler_params=limit(4),
    )(in_hbm(panels))


def operands(value):
    width = value.shape[1] // 2
    lane = lax.broadcasted_iota(jnp.int32, value.shape, 1)
    high = value.astype(jnp.bfloat16)
    as_wide = high.astype(jnp.float32)
    return jnp.where(lane < width, as_wide, value - as_wide).astype(jnp.bfloat16), high


def applied(matrix_high, matrix_low, both, high):
    first = jnp.dot(matrix_high, both, preferred_element_type=jnp.float32)
    second = jnp.dot(matrix_low, high, preferred_element_type=jnp.float32)
    return (first + pltpu.roll(first, first.shape[1] // 2, 1)) + second


def doubled(value):
    return jnp.concatenate([value, value], axis=0).T


def left_of(own_rhs, parts):
    total = parts[0][...]
    for part in parts[1:]:
        total = total + part[...]
    return own_rhs[...] - total


def sum_kernel(first, second, out):
    out[...] = first[...] + second[...]


def pending_sum(first, second):
    return pl.pallas_call(
        sum_kernel,
        out_shape=shaped(*first.shape),
        in_specs=[VMEM, VMEM],
        out_specs=VMEM,
        cost_estimate=cost(first.shape[1] ** 2 * 256),
        compiler_params=limit(4),
    )(first, second)


def direct_kernel(tier, count, where, own_rhs, halves, *refs):
    parts, (left, term) = refs[:count], refs[count:]

    @pl.when(where[2] == tier)
    def _():
        left[...] = left_of(own_rhs, parts)
        value = applied(halves[0], halves[1], *operands(doubled(left[...])))
        term[...] = value.T[: term.shape[0]]


def direct(where, tier, own_rhs, halves, parts):
    width, rows = own_rhs.shape
    return pl.pallas_call(
        functools.partial(direct_kernel, tier, len(parts)),
        out_shape=(shaped(width, rows), shaped(width, rows)),
        in_specs=[SMEM] + [VMEM] * (2 + len(parts)),
        out_specs=(VMEM, VMEM),
        cost_estimate=cost(rows**2 * 64),
        compiler_params=limit(8),
    )(where, own_rhs, in_vmem(halves), *parts)


def tail_of(copies, held, both, high, width, out):
    rows = held.shape[0]
    block = rows // 4
    for at in range(0, rows, block):
        part = slice(at, at + block)
        if copies:
            wait(copies, part)
        out[:width, part] = applied(*split(held[part]), both, high).T[:width]


def with_squares(out, width, squares):
    out[width:, :] = jnp.zeros((8, out.shape[1]), jnp.float32)
    out[width:, : squares.shape[1]] = squares[...]


def solve_kernel(tier, last, with_tail, where, left, halves, solved, *refs):
    panel, refs = refs[0] if with_tail else None, refs[with_tail:]
    out, squares, kept, *sent = refs
    width = left.shape[0]

    @pl.when(where[2] != tier)
    def _():
        out[...] = solved[...]

    @pl.when(where[2] == tier)
    def _():
        value = applied(halves[2], halves[3], *operands(doubled(left[...])))
        out[...] = value.T[:width]
        kept[...] = value
        own = jnp.sum(value * value, axis=0, keepdims=True)
        squares[...] = jnp.broadcast_to(own, squares.shape)
        if sent:
            tail_of(None, panel, *operands(value), width, sent[0])
            if last:
                with_squares(sent[0], width, squares)


def solve(where, tier, left, halves, solved, panel=None, last=False):
    width, rows = left.shape
    with_tail = panel is not None
    return pl.pallas_call(
        functools.partial(solve_kernel, tier, last, with_tail),
        out_shape=[shaped(width, rows), shaped(8, 2 * width), shaped(rows, 2 * width)]
        + [shaped(width + 8 * last, rows)] * with_tail,
        in_specs=[SMEM] + [VMEM] * (3 + with_tail),
        out_specs=[VMEM] * (3 + with_tail),
        cost_estimate=cost(1),
        compiler_params=limit(8),
    )(where, left, in_vmem(halves), solved, *([in_vmem(panel)] if with_tail else []))


def tails_kernel(tier, where, value, squares, panels, *refs):
    sent, (held, arrived) = refs[:-2], refs[-2:]
    width = squares.shape[1] // 2

    @pl.when(where[2] == tier)
    def _():
        copies = [
            pieces(panels.at[0, 2 + step], held.at[step], arrived.at[step])
            for step in range(held.shape[0])
        ]
        both, high = operands(value[...])
        for step, out in enumerate(sent):
            tail_of(copies[step], held.at[step], both, high, width, out)
        with_squares(sent[-1], width, squares)


def more_tails(where, tier, value, squares, panels, count):
    rows = value.shape[0]
    width = squares.shape[1] // 2
    shapes = [(width + 8 * (step == count - 1), rows) for step in range(count)]
    return pl.pallas_call(
        functools.partial(tails_kernel, tier),
        out_shape=[shaped(*shape) for shape in shapes],
        in_specs=[SMEM, VMEM, VMEM, HBM],
        out_specs=[VMEM] * count,
        scratch_shapes=[
            pltpu.VMEM((count, rows, rows), jnp.float32),
            pltpu.SemaphoreType.DMA((count, rows // PIECE)),
        ],
        cost_estimate=cost(1),
        compiler_params=limit(8 + 4 * count),
    )(where, value, squares, in_hbm(panels))


def last_kernel(leaves, count, where, own_rhs, halves, squares, got, first, second, kept, widths):

    @pl.when(where[1] != leaves - 1)
    def _():
        widths[...] = jnp.zeros_like(widths)

    @pl.when(where[1] == leaves - 1)
    def _():
        left = left_of(own_rhs, (first, second))
        value = applied(halves[2], halves[3], *operands(doubled(left)))
        kept[...] = value
        total = (squares[...] + got[...]) + jnp.sum(value * value, axis=0, keepdims=True)
        widths[...] = jnp.sqrt(total / count + 1e-06)


def last(leaves, count, where, own_rhs, halves, squares, got, parts):
    width, rows = own_rhs.shape
    return pl.pallas_call(
        functools.partial(last_kernel, leaves, count),
        out_shape=(shaped(rows, 2 * width), shaped(*squares.shape)),
        in_specs=[SMEM] + [VMEM] * 6,
        out_specs=(VMEM, VMEM),
        cost_estimate=cost(1),
        compiler_params=limit(8),
    )(where, own_rhs, in_vmem(halves), squares, got, *parts)


def settle_kernel(tiers, where, solved, value, out):
    width = out.shape[0]

    @pl.when(where[2] == tiers)
    def _():
        out[...] = value[...].T[:width]

    @pl.when(where[2] != tiers)
    def _():
        out[...] = solved[...]


def settled(tiers, where, solved, value):
    return pl.pallas_call(
        functools.partial(settle_kernel, tiers),
        out_shape=shaped(*solved.shape),
        in_specs=[SMEM, VMEM, VMEM],
        out_specs=VMEM,
        cost_estimate=cost(1),
        compiler_params=limit(6),
    )(where, solved, value)


def local(rhs_rows, order, leaf_inverse, leaf_panels, panel_mask, sep_rhs, sep_inverse, sep_panels):
    n_leaf = lax.axis_size("leaf")
    n_grid = lax.axis_size("grid")
    tiers = leaf_panels.shape[1]
    block_rows, columns = rhs_rows.shape
    block_count = n_leaf * n_grid
    sep_rows = sep_rhs.shape[1]
    width = columns // n_grid
    leaf = lax.axis_index("leaf").astype(jnp.int32)
    grid = lax.axis_index("grid").astype(jnp.int32)
    level = jnp.ones((), jnp.int32)
    for bit in range(1, tiers):
        level = level + ((leaf + 1) & (2**bit - 1) == 0).astype(jnp.int32)
    where = jnp.stack([grid, leaf, level])
    scale = jnp.repeat(panel_mask[0].astype(jnp.float32), 128, axis=1)

    picked = pick(rhs_rows, order)
    picked, where = lax.optimization_barrier((picked, where))
    moved = lax.all_to_all(
        picked.reshape(block_count, block_rows // block_count, columns),
        ("leaf", "grid"),
        split_axis=0,
        concat_axis=0,
        tiled=True,
    )
    permuted = moved.reshape(block_rows, columns)

    _, inverse, own_panels = lax.optimization_barrier((picked, sep_inverse, sep_panels))
    halves = prepared(inverse, own_panels)
    permuted, halves = lax.optimization_barrier((permuted, halves))

    given, kept = two_products(where, leaf_inverse, permuted, True)
    in_chip = lax.ppermute(given, "grid", [(0, 1), (1, 0), (2, 3)])
    onward = kept + in_chip
    onward, permuted, halves = lax.optimization_barrier((onward, permuted, halves))
    between = lax.ppermute(onward, "grid", [(0, 2), (1, 3)])
    *low_block, lowest = two_products(where, leaf_inverse, permuted, False)
    from_pair = [lax.ppermute(part, "grid", [(0, 1)]) for part in low_block]
    halves, panels = loaded(halves, leaf_panels)

    leaf_y, turned, squares, given, kept = first_update(
        where, (kept, in_chip, between, lowest, *low_block, *from_pair), scale, panels
    )
    swap = [(0, 1), (1, 0), (2, 3), (3, 2)]
    over = [(0, 2), (1, 3), (2, 0), (3, 1)]
    got = lax.ppermute(given, "grid", swap)
    given, other = second_update(where, turned, scale, panels)
    own, away = chip_sum(where, kept, got)
    away, given, turned = lax.optimization_barrier((away, given, turned))
    got = lax.ppermute(away, "grid", over)
    second, away = chip_sum(where, other, lax.ppermute(given, "grid", swap))
    given, kept = later_updates(where, squares, turned, scale, panels)
    got, away, given = lax.optimization_barrier((got, away, given))
    mine = own + got
    following = second + lax.ppermute(away, "grid", over)
    own, away = chip_sum(where, kept, lax.ppermute(given, "grid", swap))
    pairs = [(base + 1, base) for base in range(0, n_leaf, 2)]
    own, own_panels = lax.optimization_barrier((own, sep_panels))
    next_panel = loaded_panel(own_panels)
    got, own, next_panel = lax.optimization_barrier(
        (lax.ppermute(mine, "leaf", pairs), own, next_panel)
    )
    parts = [mine, got]
    edges = [(step * width, (step + 1) * width) for step in range(tiers - 2)]
    edges[-1] = (edges[-1][0], own.shape[0])
    rest = [
        own[start:stop] + lax.ppermute(away[start:stop], "grid", over) for start, stop in edges
    ]

    own_rhs = sep_rhs[0].T
    solved = jnp.zeros_like(own_rhs)
    waiting = []
    for tier in range(1, tiers):
        size = 2**tier
        direct_left, direct_right, early, onward, aside = [], [], [], [], []
        for base in range(0, n_leaf, size):
            host, end = (base + size // 2 - 1, base + size - 1)
            parent = base // (2 * size) * 2 * size + size - 1
            onward.append((host, end))
            if end == parent:
                direct_left.append((host, parent))
            else:
                direct_right.append((host, parent))
                early.append((end, parent))
                aside.append((host, end))
        left, term = direct(where, tier, own_rhs, halves, parts)
        count = len(rest)
        solved, own, *more = solve(
            where, tier, left, halves, solved, next_panel if count else None, count == 1
        )
        if waiting:
            _, following, *waiting = lax.optimization_barrier((left, following, *waiting))
            rest = [
                other + lax.ppermute(other + tail, "leaf", before)
                for other, tail in zip(rest, waiting)
            ]
        if count:
            value, tail = more
            term = following + term
            from_left = lax.ppermute(term, "leaf", direct_left)
            if tier == 1:
                turn, tail = lax.optimization_barrier((lax.ppermute(term, "leaf", aside), tail))
                parts = [following, lax.ppermute(following + turn, "leaf", early), from_left]
            else:
                next_early = lax.ppermute(following, "leaf", early)
                from_right = lax.ppermute(term, "leaf", direct_right)
                parts = [pending_sum(following, next_early), from_left, from_right]
            following = rest[0] + lax.ppermute(rest[0] + tail, "leaf", onward)
            rest = rest[1:]
            waiting = []
            if count > 1:
                value, _ = lax.optimization_barrier((value, from_left))
                waiting = more_tails(where, tier, value, own, sep_panels, count - 1)
                parts[1], *waiting = lax.optimization_barrier((parts[1], *waiting))
            before = onward
        else:
            squares = following[width:, : 2 * width]
            following = following[:width]
            parts = [following, lax.ppermute(following + term, "leaf", direct_left)]
            got = lax.ppermute(squares + own, "leaf", direct_left)
    value, widths = last(
        n_leaf,
        n_leaf * (block_rows * n_grid + sep_rows),
        where,
        own_rhs,
        halves,
        squares,
        got,
        parts,
    )
    solved = settled(tiers, where, solved, value)
    step = n_leaf
    while step > 1:
        half_step = step // 2
        steps = [(end, end - half_step) for end in range(step - 1, n_leaf, step)]
        widths = widths + lax.ppermute(widths, "leaf", steps)
        step = half_step
    return (leaf_y, solved.T[None], widths[0, :width])


def solution(mesh):
    placed = (
        P(("leaf", "grid"), None),
        P(("leaf", "grid")),
        P("leaf", "grid"),
        P("leaf", None, None, "grid"),
        P("leaf", None, "grid"),
        P("leaf", None, "grid"),
        P("leaf", None, None),
        P("leaf", None, None, None),
    )
    return jax.shard_map(
        local,
        mesh=mesh,
        in_specs=placed,
        out_specs=(P(("leaf", "grid"), None), P("leaf", None, "grid"), P("grid")),
        check_vma=False,
    )
```
